256 devices in a mesh: ctx: 32 (over z_hi, y, core), tp: 8 (over z_lo, x).
Axes of the slice: x: 4, y: 4, z: 8 (z_hi: 4, z_lo: 2; z = z_hi * 2 + z_lo), core: 2. Of those that a mesh axis runs over, the one named last changes fastest.
Arguments:
- q_proj: bfloat16 [8192, 8192], P('ctx', 'tp'), may hold values from -6 to 6
- k_proj: bfloat16 [8192, 8192], P('ctx', 'tp'), may hold values from -6 to 6
- v_proj: bfloat16 [8192, 8192], P('ctx', 'tp'), may hold values from -6 to 6
- filters: float32 [8192, 512], P('ctx', 'tp'), may hold values from -0.0625 to 0.0625
- lengths: int32 [512], P('tp'), may hold values from 1 to 8192, as said below
- skip_gain: float32 [8192], P('tp'), may hold values from -4 to 4
- out_weight: bfloat16 [8192, 4096], P('tp'), may hold values from -0.0625 to 0.0625
Outputs:
- projected: bfloat16 [8192, 4096], P(('ctx', 'tp'))
The draws below stay inside these ranges and needn't reach their ends.
Inputs may be any that keep to these rules, and one draw needn't show every extreme that they name: `lengths`: some group's filter has exactly 8192 taps and some group's exactly 1.
All inputs are finite; a program needn't handle non-finite values.
Results may differ from the reference program's by a relative error of at most 0.014.
Values may be sent and summed in bfloat16 or wider, within the bound.
A program may use at most 128 MiB of HBM per device.

```python
import jax
import jax.numpy as jnp
from jax import lax

D = 8192
OUT = 4096
GROUP = 16
TOKENS = 8192
GROUPS = 512


def draw_lengths(key, part):
    key = jax.random.fold_in(key, 11)
    first_key, second_key = jax.random.split(key)
    drawn_lengths = jax.random.randint(first_key, (GROUPS,), 1, TOKENS + 1)
    chosen = jax.random.permutation(second_key, GROUPS)
    indices = jnp.arange(GROUPS)
    drawn_lengths = jnp.where(indices == chosen[0], TOKENS, drawn_lengths)
    drawn_lengths = jnp.where(indices == chosen[1], 1, drawn_lengths)
    return drawn_lengths.astype(jnp.int32)


def shard_levels(key, shape, cuts, smallest, top_value):
    def one(axis_at, shards_of):
        steps = jax.random.uniform(jax.random.fold_in(jax.random.fold_in(key, 6), axis_at), (shards_of,), jnp.float32, smallest / len(cuts), top_value / len(cuts))
        return jnp.repeat(jnp.exp(steps), shape[axis_at] // shards_of).reshape((-1,) + (1,) * (len(shape) - axis_at - 1))

    gain = one(*cuts[0])
    for cut in cuts[1:]:
        gain = gain * one(*cut)
    return gain


def normal_values(rng, dims, scale, most, pieces=(), kind=jnp.bfloat16):
    values = jax.random.normal(rng, dims, jnp.float32) * scale
    if len(pieces) > 0:
        values = shard_levels(rng, dims, pieces, -0.22, 0.18) * values
    return jnp.clip(values, min=-most, max=most).astype(kind)


def setup_inputs(seed: int = 0) -> dict:
    key_list = jax.random.split(jax.random.key(seed), 8)
    q_proj = normal_values(key_list[0], (TOKENS, D), 1.0, 6.0, ((0, 32), (1, 8)))
    k_proj = normal_values(key_list[1], (TOKENS, D), 1.0, 6.0, ((0, 32), (1, 8)))
    v_proj = normal_values(key_list[2], (TOKENS, D), 1.0, 6.0, ((0, 32), (1, 8)))
    filters = normal_values(key_list[3], (TOKENS, GROUPS), TOKENS ** -0.5, 0.0625, ((0, 32), (1, 8)), jnp.float32)
    lengths = draw_lengths(jax.random.fold_in(key_list[7], 71), 0)
    skip_gain = normal_values(key_list[5], (D,), 1.0, 4.0, ((0, 8),), jnp.float32)
    out_weight = normal_values(key_list[6], (D, OUT), D ** -0.5, 0.0625, ((0, 8),))
    return dict(q_proj=q_proj, k_proj=k_proj, v_proj=v_proj, filters=filters, lengths=lengths, skip_gain=skip_gain, out_weight=out_weight)


def convolve(inputs_pair):
    signal, kernel = inputs_pair
    full_length = 2 * TOKENS
    spectrum = jnp.fft.rfft(signal, n=full_length, axis=0) * jnp.fft.rfft(kernel, n=full_length, axis=0)[:, :, None]
    return jnp.fft.irfft(spectrum, n=full_length, axis=0)[:TOKENS]


def reference(q_proj, k_proj, v_proj, filters, lengths, skip_gain, out_weight):
    gated = (k_proj.astype(jnp.float32) * v_proj.astype(jnp.float32)).astype(jnp.bfloat16)
    positions = jnp.arange(TOKENS, dtype=jnp.int32)[:, None]
    masked = jnp.where(positions < lengths[None, :], filters, jnp.zeros_like(filters))
    per_block = 32 if GROUPS % 32 == 0 else GROUPS
    blocks = GROUPS // per_block
    signal_blocks = gated.astype(jnp.float32).reshape(TOKENS, blocks, per_block, GROUP).transpose(1, 0, 2, 3)
    kernel_blocks = masked.reshape(TOKENS, blocks, per_block).transpose(1, 0, 2)
    conv_field = lax.map(convolve, (signal_blocks, kernel_blocks))
    conv_field = conv_field.transpose(1, 0, 2, 3).reshape(TOKENS, D)
    mixed_rows = (q_proj.astype(jnp.float32) * (conv_field + skip_gain[None, :] * gated.astype(jnp.float32))).astype(jnp.bfloat16)
    return jnp.dot(mixed_rows, out_weight, preferred_element_type=jnp.float32).astype(jnp.bfloat16)
```

```python
import functools

import jax
import jax.numpy as jnp
import numpy as np
from jax import lax
from jax.experimental import pallas as pl
from jax.experimental.pallas import tpu as pltpu
from jax.sharding import PartitionSpec as P

MESH = pl.DeviceIdType.MESH
BF = jnp.bfloat16
F32 = jnp.float32

CTX = 32
TOK = 256
CH = 1024
GRP = 64
C16 = 16
OUT = 4096
HALF = OUT // 2
R = 32
Q = 8
RC = R // 2
SEQ = CTX * TOK
WIDE = SEQ + 256

ORDER = (0, 2, 4, 6, 1, 3, 5, 7)
PLACE = tuple(ORDER.index(i) for i in range(8))


def lane_swap():
    swap = np.zeros((8, 8, 16, 8, 8, 16), np.float32)
    for a in range(8):
        for b in range(8):
            for c in range(16):
                swap[a, b, c, PLACE[b], a, c] = 1.0
    return swap.reshape(CH, CH)


def exact_dot(left, right):
    return jnp.dot(left, right, preferred_element_type=F32)


def kernel(
    k_hbm, v_hbm, q_hbm, f_hbm, w_hbm, s_hbm, lens, skip, out,
    kbuf, vbuf, qbuf, fbuf, wbuf, swap, gated, stage,
    fsend, frecv, xsend, xrecv, wide, toep, xpad, xv, yacc, ysend, yrecv, mixed,
    za, zb, ra, rb, sa, sb, r2a, r2b,
    load_sem, f_sem, x_sem, y_sem, rs_send, rs_recv,
):
    me = lax.axis_index("ctx")
    tp = lax.axis_index("tp")
    zl, x = tp // 4, lax.rem(tp, 4)
    other = {"tp": (1 - zl) * 4 + x}

    def along_x(step):
        return {"tp": zl * 4 + lax.rem(x + step, 4)}

    barrier = pltpu.get_barrier_semaphore()

    @pl.loop(1, CTX)
    def _(step):
        pl.semaphore_signal(
            barrier, inc=1, device_id={"ctx": lax.rem(me + step, CTX)}, device_id_type=MESH
        )

    for step in (1, 2, 3):
        pl.semaphore_signal(barrier, inc=1, device_id=along_x(step), device_id_type=MESH)
    pl.semaphore_signal(barrier, inc=1, device_id=other, device_id_type=MESH)

    def load(source, target, index):
        copy = pltpu.make_async_copy(source, target, load_sem.at[index])
        copy.start()
        return copy

    f_load = load(f_hbm, fbuf, 0)
    k_load = load(k_hbm, kbuf, 1)
    v_load = load(v_hbm, vbuf, 2)
    s_load = load(s_hbm, swap, 3)
    q_load = load(q_hbm, qbuf, 4)
    w_load = load(w_hbm, wbuf, 5)

    f_load.wait()
    lag = me * TOK + lax.broadcasted_iota(jnp.int32, (TOK, GRP), 0)
    taps = jnp.where(lag < lens[...], fbuf[...], 0.0).astype(BF)
    row = lax.broadcasted_iota(jnp.int32, (TOK, TOK), 0)
    col = lax.broadcasted_iota(jnp.int32, (TOK, TOK), 1)
    flip = jnp.where(row + col == TOK - 1, 1.0, 0.0).astype(BF)
    back = lax.dot_general(
        taps, flip, (((0,), (0,)), ((), ())), preferred_element_type=F32
    ).astype(BF)
    row = lax.broadcasted_iota(jnp.int32, (128, GRP), 0)
    col = lax.broadcasted_iota(jnp.int32, (128, GRP), 1)
    rows = None
    for half in range(2):
        pick = jnp.where(row == 2 * col + half, 1.0, 0.0).astype(BF)
        part = exact_dot(pick, back[:, half * 128 : half * 128 + 128])
        rows = part if rows is None else rows + part
    for e in range(CTX):
        fsend[e] = rows[4 * e : 4 * e + 4]
    frecv[me] = fsend[me]

    pl.semaphore_wait(barrier, CTX - 1 + 4)

    def send_all(source, target, sems):
        @pl.loop(1, CTX)
        def _(step):
            e = lax.rem(me + step, CTX)
            pltpu.make_async_remote_copy(
                source.at[e], target.at[me], sems.at[0], sems.at[1],
                device_id={"ctx": e}, device_id_type=MESH,
            ).start()

    def waiter(source, target, sems):
        return pltpu.make_async_remote_copy(
            source.at[pl.ds(0, CTX - 1)], target.at[pl.ds(0, CTX - 1)], sems.at[0], sems.at[1],
            device_id={"ctx": lax.rem(me + 1, CTX)}, device_id_type=MESH,
        )

    send_all(fsend, frecv, f_sem)

    k_load.wait()
    v_load.wait()
    for i in range(Q):
        part = (kbuf[i * R : i * R + R].astype(F32) * vbuf[i * R : i * R + R].astype(F32)).astype(BF)
        gated[i * R : i * R + R] = part
        for o in range(8):
            stage[o * R : o * R + R, i * 128 : i * 128 + 128] = part[:, o * 128 : o * 128 + 128]
    s_load.wait()
    for g in range(2):
        packed = exact_dot(stage[...], swap[:, g * 512 : g * 512 + 512]).astype(BF)
        for o in range(8):
            for i in range(4):
                xsend[g, o * 4 + i] = packed[o * R : o * R + R, i * 128 : i * 128 + 128]
        xrecv[g, me] = xsend[g, me]
        send_all(xsend.at[g], xrecv.at[g], x_sem.at[g])

    waiter(fsend, frecv, f_sem).wait_recv()
    for g in range(2):
        for n in range(2 * CTX):
            tap_row = frecv[CTX - 1 - n // 2, g * 2 + n % 2 : g * 2 + n % 2 + 1, :]
            wide[:, n * 128 : n * 128 + 128] = jnp.broadcast_to(tap_row, (8, 128))
        wide[:, SEQ:] = jnp.zeros((8, WIDE - SEQ), F32)
        wide[...] = pltpu.roll(wide[...], WIDE - 7, 1, stride=1, stride_axis=0)

        @pl.loop(0, 8)
        def _(a):
            whole = wide[...]
            high = pltpu.roll(whole, WIDE - 120 + 16 * a, 1)
            low = pltpu.roll(whole, WIDE - 112 + 16 * a, 1)
            both = jnp.concatenate([high, low], axis=0).astype(BF)
            at = pl.multiple_of(a * 16, 16)
            toep[g, pl.ds(at + 128, 16), :] = both[:, :SEQ]
            toep[g, pl.ds(at, 16), :] = both[:, 128 : SEQ + 128]

    xpad[:, :128] = jnp.zeros((TOK, 128), BF)
    for g in range(2):
        waiter(xsend.at[g], xrecv.at[g], x_sem.at[g]).wait_recv()
        for b in range(CTX):
            stage[(b // 8) * R : (b // 8) * R + R, (b % 8) * 128 : (b % 8) * 128 + 128] = xrecv[g, b]
        blocks = exact_dot(stage[:128, :], swap[...]).astype(BF)
        for o in range(4):
            for i in range(Q):
                xpad[i * R : i * R + R, 128 + o * 128 : 256 + o * 128] = blocks[
                    o * R : o * R + R, PLACE[i] * 128 : PLACE[i] * 128 + 128
                ]
        for n in range(8):
            moved = xpad[...]
            if n < 7:
                moved = pltpu.roll(moved, 16 * (7 - n), 1)
            xv[n * TOK : n * TOK + TOK, :] = moved[:, 128:]
        for d in range(4):
            width = 512 - 128 * d
            part = exact_dot(toep[g, :, (24 - 8 * d) * TOK : (32 - 8 * d) * TOK], xv[:, :width])
            if d == 0:
                yacc[g] = part
            else:
                yacc[g, :, 128 * d :] = yacc[g, :, 128 * d :] + part

    for ck in range(2):
        for g in range(2):
            for o in range(4):
                for i in range(Q):
                    at = i * R + ck * RC
                    stage[g * 64 + o * RC : g * 64 + o * RC + RC, i * 128 : i * 128 + 128] = yacc[
                        g, at : at + RC, o * 128 : o * 128 + 128
                    ].astype(BF)
        packed = exact_dot(stage[:128, :], swap[...]).astype(BF)
        for g in range(2):
            for b in range(CTX):
                at = g * 64 + (b // 8) * RC
                lane = PLACE[b % 8] * 128
                ysend[ck, b, g] = packed[at : at + RC, lane : lane + 128]
        yrecv[ck, me] = ysend[ck, me]
        send_all(ysend.at[ck], yrecv.at[ck], y_sem.at[ck])

    def rs_copy(source, target, index, device):
        return pltpu.make_async_remote_copy(
            source, target, rs_send.at[index], rs_recv.at[index], device_id=device, device_id_type=MESH
        )

    def first_a(ck, step):
        return rs_copy(za.at[ck, lax.rem(x + step, 4)], ra.at[ck, step - 1], ck * 8 + step - 1, along_x(step))

    def first_b(ck):
        return rs_copy(zb.at[ck, 1 - zl], rb.at[ck], ck * 8 + 3, other)

    def second_a(ck):
        return rs_copy(sa.at[ck, 1 - zl], r2a.at[ck], ck * 8 + 4, other)

    def second_b(ck, step):
        return rs_copy(
            sb.at[ck, lax.rem(x + step, 4)], r2b.at[ck, step - 1], ck * 8 + 4 + step, along_x(step)
        )

    q_load.wait()
    w_load.wait()
    for ck in range(2):
        waiter(ysend.at[ck], yrecv.at[ck], y_sem.at[ck]).wait_recv()
        for e in range(CTX):
            for g in range(2):
                o, i = e // 4, (e % 4) * 2 + g
                stage[o * RC : o * RC + RC, i * 128 : i * 128 + 128] = yrecv[ck, e, g]
        field = exact_dot(stage[:128, :], swap[...])
        for i in range(Q):
            at = i * R + ck * RC
            for o in range(8):
                lane = slice(o * 128, o * 128 + 128)
                conv = field[o * RC : o * RC + RC, PLACE[i] * 128 : PLACE[i] * 128 + 128]
                direct = skip[:, lane] * gated[at : at + RC, lane].astype(F32)
                mixed[i * RC : i * RC + RC, lane] = (
                    qbuf[at : at + RC, lane].astype(F32) * (conv + direct)
                ).astype(BF)

        @pl.loop(0, HALF // 512)
        def _(t):
            cols = pl.ds(pl.multiple_of(t * 512, 512), 512)
            cols_b = pl.ds(pl.multiple_of(t * 512 + HALF, 512), 512)
            part = exact_dot(mixed[...], wbuf[:, cols]).astype(BF)
            part_b = exact_dot(mixed[...], wbuf[:, cols_b]).astype(BF)
            for p in range(8):
                za[ck, p % 4, p // 4, :, cols] = part[p * RC : p * RC + RC]
                zb[ck, p // 4, p % 4, :, cols] = part_b[p * RC : p * RC + RC]

        for step in (1, 2, 3):
            first_a(ck, step).start()
        first_b(ck).start()

    for ck in range(2):
        first_b(ck).wait_recv()
        for i in range(4):
            sb[ck, i] = (zb[ck, zl, i].astype(F32) + rb[ck, i].astype(F32)).astype(BF)
        for step in (1, 2, 3):
            second_b(ck, step).start()
        for step in (1, 2, 3):
            first_a(ck, step).wait_recv()
        for i in range(2):
            total = za[ck, x, i].astype(F32)
            for step in range(3):
                total = total + ra[ck, step, i].astype(F32)
            sa[ck, i] = total.astype(BF)
        second_a(ck).start()

    for ck in range(2):
        rows = slice(ck * RC, ck * RC + RC)
        second_a(ck).wait_recv()
        out[rows, :HALF] = (sa[ck, zl].astype(F32) + r2a[ck].astype(F32)).astype(BF)
        for step in (1, 2, 3):
            second_b(ck, step).wait_recv()
        total = sb[ck, x].astype(F32)
        for step in range(3):
            total = total + r2b[ck, step].astype(F32)
        out[rows, HALF:] = total.astype(BF)

    waiter(fsend, frecv, f_sem).wait_send()
    for i in range(2):
        waiter(xsend.at[i], xrecv.at[i], x_sem.at[i]).wait_send()
        waiter(ysend.at[i], yrecv.at[i], y_sem.at[i]).wait_send()
        for step in (1, 2, 3):
            first_a(i, step).wait_send()
            second_b(i, step).wait_send()
        first_b(i).wait_send()
        second_a(i).wait_send()


def shards(q_proj, k_proj, v_proj, filters, lengths, skip_gain, out_weight):
    swap = jnp.asarray(lane_swap(), BF)
    vmem = pl.BlockSpec(memory_space=pltpu.VMEM)
    hbm = pl.BlockSpec(memory_space=pl.ANY)
    dma = pltpu.SemaphoreType.DMA
    scratch = [
        pltpu.VMEM((TOK, CH), BF),
        pltpu.VMEM((TOK, CH), BF),
        pltpu.VMEM((TOK, CH), BF),
        pltpu.VMEM((TOK, GRP), F32),
        pltpu.VMEM((CH, OUT), BF),
        pltpu.VMEM((CH, CH), BF),
        pltpu.VMEM((TOK, CH), BF),
        pltpu.VMEM((TOK, CH), BF),
        pltpu.VMEM((CTX, 4, 128), F32),
        pltpu.VMEM((CTX, 4, 128), F32),
        pltpu.VMEM((2, CTX, R, 128), BF),
        pltpu.VMEM((2, CTX, R, 128), BF),
        pltpu.VMEM((8, WIDE), F32),
        pltpu.VMEM((2, TOK, SEQ), BF),
        pltpu.VMEM((TOK, 640), BF),
        pltpu.VMEM((8 * TOK, 512), BF),
        pltpu.VMEM((2, TOK, 512), F32),
        pltpu.VMEM((2, CTX, 2, RC, 128), BF),
        pltpu.VMEM((2, CTX, 2, RC, 128), BF),
        pltpu.VMEM((128, CH), BF),
        pltpu.VMEM((2, 4, 2, RC, HALF), BF),
        pltpu.VMEM((2, 2, 4, RC, HALF), BF),
        pltpu.VMEM((2, 3, 2, RC, HALF), BF),
        pltpu.VMEM((2, 4, RC, HALF), BF),
        pltpu.VMEM((2, 2, RC, HALF), BF),
        pltpu.VMEM((2, 4, RC, HALF), BF),
        pltpu.VMEM((2, RC, HALF), BF),
        pltpu.VMEM((2, 3, RC, HALF), BF),
        dma((6,)),
        dma((2,)),
        dma((2, 2)),
        dma((2, 2)),
        dma((16,)),
        dma((16,)),
    ]
    return pl.pallas_call(
        kernel,
        out_shape=jax.ShapeDtypeStruct((R, OUT), BF),
        in_specs=[hbm] * 6 + [vmem] * 2,
        out_specs=vmem,
        scratch_shapes=scratch,
        compiler_params=pltpu.CompilerParams(
            collective_id=0, has_side_effects=True, vmem_limit_bytes=56 << 20
        ),
        name="hyena",
    )(
        k_proj, v_proj, q_proj, filters, out_weight, swap,
        lengths.reshape(1, GRP), skip_gain.reshape(1, CH),
    )


def solution(mesh):
    return jax.shard_map(
        shards,
        mesh=mesh,
        in_specs=(
            P("ctx", "tp"),
            P("ctx", "tp"),
            P("ctx", "tp"),
            P("ctx", "tp"),
            P("tp"),
            P("tp"),
            P("tp", None),
        ),
        out_specs=P(("ctx", "tp"), None),
        check_vma=False,
    )
```

```python
import functools

import jax
import jax.numpy as jnp
import numpy as np
from jax import lax
from jax.experimental import pallas as pl
from jax.experimental.pallas import tpu as pltpu
from jax.sharding import PartitionSpec as P

MESH = pl.DeviceIdType.MESH
BF = jnp.bfloat16
F32 = jnp.float32

CTX = 32
TOK = 256
CH = 1024
GRP = 64
C16 = 16
OUT = 4096
R = 32
Q = 8
RC = R // 2
SEQ = CTX * TOK
WIDE = SEQ + 256

ORDER = (0, 2, 4, 6, 1, 3, 5, 7)
PLACE = tuple(ORDER.index(i) for i in range(8))


ROUTES = (
    (0, 1280, ("x0", "x1", "z")),
    (1280, 1536, ("x1", "z", "x0")),
    (2816, 1280, ("z", "x0", "x1")),
)


def bit(tp, way):
    x = tp % 4
    if way == "z":
        return tp // 4
    return x // 2 if way == "x1" else (x + 1) // 2 % 2


def lane_swap():
    swap = np.zeros((8, 8, 16, 8, 8, 16), np.float32)
    for a in range(8):
        for b in range(8):
            for c in range(16):
                swap[a, b, c, PLACE[b], a, c] = 1.0
    return swap.reshape(CH, CH)


def exact_dot(left, right):
    return jnp.dot(left, right, preferred_element_type=F32)


def kernel(
    k_hbm, v_hbm, q_hbm, f_hbm, w_hbm, s_hbm, l_hbm, d_hbm, out,
    kbuf, vbuf, qbuf, fbuf, wbuf, swap, lens, skip, gated, stage,
    fsend, frecv, xsend, xrecv, wide, toep, xpad, xv, yacc, y0send, y0recv, y1send, y1recv, q_own, direct, mixed, zacc,
    *rest,
):
    sums, (load_sem, f_sem, x_sem, y_sem, rs_send, rs_recv) = rest[:-6], rest[-6:]
    me = lax.axis_index("ctx")
    tp = lax.axis_index("tp")
    zl, x = tp // 4, lax.rem(tp, 4)
    mine = {"x0": lax.rem((x + 1) // 2, 2), "x1": x // 2, "z": zl}
    partner = {
        "x0": {"tp": zl * 4 + x + 1 - 2 * lax.rem(x, 2)},
        "x1": {"tp": zl * 4 + 3 - x},
        "z": {"tp": (1 - zl) * 4 + x},
    }

    def load(source, target, index):
        copy = pltpu.make_async_copy(source, target, load_sem.at[index])
        copy.start()
        return copy

    k_load = load(k_hbm, kbuf, 0)
    v_load = load(v_hbm, vbuf, 1)
    s_load = load(s_hbm, swap, 2)
    f_load = load(f_hbm, fbuf, 3)
    l_load = load(l_hbm, lens, 4)
    d_load = load(d_hbm, skip, 5)

    barrier = pltpu.get_barrier_semaphore()

    @pl.loop(1, CTX)
    def _(step):
        pl.semaphore_signal(
            barrier, inc=1, device_id={"ctx": lax.rem(me + step, CTX)}, device_id_type=MESH
        )

    for way in ("x0", "x1", "z"):
        pl.semaphore_signal(barrier, inc=1, device_id=partner[way], device_id_type=MESH)

    def send_all(source, target, sems):
        for far in (2, 1, 3, 0):

            @pl.loop(0 if far else 1, 8)
            def _(near):
                e = lax.rem(me // 8 + far, 4) * 8
                e += lax.rem(me // 2 + near // 2, 4) * 2 + lax.rem(me + near, 2)
                pltpu.make_async_remote_copy(
                    source.at[e], target.at[me], sems.at[0], sems.at[1],
                    device_id={"ctx": e}, device_id_type=MESH,
                ).start()

    def waiter(source, target, sems):
        return pltpu.make_async_remote_copy(
            source.at[pl.ds(0, CTX - 1)], target.at[pl.ds(0, CTX - 1)], sems.at[0], sems.at[1],
            device_id={"ctx": lax.rem(me + 1, CTX)}, device_id_type=MESH,
        )

    k_load.wait()
    v_load.wait()
    for i in range(Q):
        part = (kbuf[i * R : i * R + R].astype(F32) * vbuf[i * R : i * R + R].astype(F32)).astype(BF)
        gated[i * R : i * R + R] = part
        for o in range(8):
            stage[o * R : o * R + R, i * 128 : i * 128 + 128] = part[:, o * 128 : o * 128 + 128]
    f_load.wait()
    l_load.wait()
    row = lax.broadcasted_iota(jnp.int32, (GRP, GRP), 0)
    col = lax.broadcasted_iota(jnp.int32, (GRP, GRP), 1)
    limit = jnp.sum(jnp.where(row == col, lens[...].astype(F32), 0.0), axis=1, keepdims=True)
    lag = (me * TOK + lax.broadcasted_iota(jnp.int32, (GRP, TOK), 1)).astype(F32)
    taps = jnp.where(lag < limit, fbuf[...], 0.0).astype(BF)
    row = lax.broadcasted_iota(jnp.int32, (TOK, TOK), 0)
    col = lax.broadcasted_iota(jnp.int32, (TOK, TOK), 1)
    flip = jnp.where(row + col == TOK - 1, 1.0, 0.0).astype(BF)
    back = exact_dot(taps, flip).astype(BF)
    row = lax.broadcasted_iota(jnp.int32, (128, GRP), 0)
    col = lax.broadcasted_iota(jnp.int32, (128, GRP), 1)
    rows = None
    for half in range(2):
        pick = jnp.where(row == 2 * col + half, 1.0, 0.0).astype(BF)
        part = exact_dot(pick, back[:, half * 128 : half * 128 + 128])
        rows = part if rows is None else rows + part
    for e in range(CTX):
        fsend[e] = rows[4 * e : 4 * e + 4]
    frecv[me] = fsend[me]

    s_load.wait()

    def send_group(g):
        packed = exact_dot(stage[...], swap[:, g * 512 : g * 512 + 512]).astype(BF)
        for o in range(8):
            for i in range(4):
                xsend[g, o * 4 + i] = packed[o * R : o * R + R, i * 128 : i * 128 + 128]
        xrecv[g, me] = xsend[g, me]
        if g == 0:
            pl.semaphore_wait(barrier, CTX - 1 + 3)
            send_all(fsend, frecv, f_sem)
        send_all(xsend.at[g], xrecv.at[g], x_sem.at[g])

    send_group(0)

    send_group(1)
    q_load = load(q_hbm, qbuf, 6)
    w_loads = [load(w_hbm.at[:, g], wbuf.at[g], 7 + g) for g in range(2)]
    waiter(fsend, frecv, f_sem).wait_recv()
    for g in range(2):
        for n in range(2 * CTX):
            tap_row = frecv[CTX - 1 - n // 2, g * 2 + n % 2 : g * 2 + n % 2 + 1, :]
            wide[:, n * 128 : n * 128 + 128] = jnp.broadcast_to(tap_row, (8, 128))
        wide[:, SEQ:] = jnp.zeros((8, WIDE - SEQ), F32)
        wide[...] = pltpu.roll(wide[...], WIDE - 7, 1, stride=1, stride_axis=0)

        @pl.loop(0, 8)
        def _(a):
            whole = wide[...]
            high = pltpu.roll(whole, WIDE - 120 + 16 * a, 1)
            low = pltpu.roll(whole, WIDE - 112 + 16 * a, 1)
            both = jnp.concatenate([high, low], axis=0).astype(BF)
            at = pl.multiple_of(a * 16, 16)
            toep[g, pl.ds(at + 128, 16), :] = both[:, :SEQ]
            toep[g, pl.ds(at, 16), :] = both[:, 128 : SEQ + 128]

    xpad[:, :128] = jnp.zeros((TOK, 128), BF)
    for g in range(2):
        waiter(xsend.at[g], xrecv.at[g], x_sem.at[g]).wait_recv()
        for b in range(CTX):
            stage[(b // 8) * R : (b // 8) * R + R, (b % 8) * 128 : (b % 8) * 128 + 128] = xrecv[g, b]
        blocks = exact_dot(stage[:128, :], swap[...]).astype(BF)
        for o in range(4):
            for i in range(Q):
                xpad[i * R : i * R + R, 128 + o * 128 : 256 + o * 128] = blocks[
                    o * R : o * R + R, PLACE[i] * 128 : PLACE[i] * 128 + 128
                ]
        for n in range(8):
            moved = xpad[...]
            if n < 7:
                moved = pltpu.roll(moved, 16 * (7 - n), 1)
            xv[n * TOK : n * TOK + TOK, :] = moved[:, 128:]
        acc = exact_dot(toep[g, :, 24 * TOK :], xv[...])
        yacc[...] = acc
        for d in range(1, 4):
            width = 512 - 128 * d
            part = exact_dot(toep[g, :, (24 - 8 * d) * TOK : (32 - 8 * d) * TOK], xv[:, :width])
            yacc[:, 128 * d :] = yacc[:, 128 * d :] + part

        for o in range(4):
            for i in range(Q):
                for ck in range(2):
                    at = i * R + ck * RC
                    to = ck * 64 + o * RC
                    stage[to : to + RC, i * 128 : i * 128 + 128] = yacc[
                        at : at + RC, o * 128 : o * 128 + 128
                    ].astype(BF)
        packed = exact_dot(stage[:128, :], swap[...]).astype(BF)
        for ck in range(2):
            for b in range(CTX):
                at = ck * 64 + (b // 8) * RC
                lane = PLACE[b % 8] * 128
                if g == 0:
                    y0send[b, ck * RC : ck * RC + RC] = packed[at : at + RC, lane : lane + 128]
                else:
                    y1send[ck, b] = packed[at : at + RC, lane : lane + 128]
            if g == 1:
                y1recv[ck, me] = y1send[ck, me]
                send_all(y1send.at[ck], y1recv.at[ck], y_sem.at[1 + ck])
        if g == 0:
            y0recv[me] = y0send[me]
            send_all(y0send, y0recv, y_sem.at[0])

    def hop(ck, t, step):
        whole, got0, kept1, got1, kept2, got2 = sums[6 * t : 6 * t + 6]
        way = ROUTES[t][2][step]
        source = (whole, kept1, kept2)[step].at[ck, 1 - mine[way]]
        target = (got0, got1, got2)[step].at[ck]
        index = (ck * 3 + t) * 3 + step
        return pltpu.make_async_remote_copy(
            source, target, rs_send.at[index], rs_recv.at[index],
            device_id=partner[way], device_id_type=MESH,
        )

    def add_up(ck, t, step):
        whole, got0, kept1, got1, kept2, got2 = sums[6 * t : 6 * t + 6]
        first, width, ways = ROUTES[t]
        own = mine[ways[step]]
        hop(ck, t, step).wait_recv()
        if step == 0:
            for i in range(2):
                for j in range(2):
                    kept1[ck, i, j] = (whole[ck, own, i, j].astype(F32) + got0[ck, i, j].astype(F32)).astype(BF)
        elif step == 1:
            for i in range(2):
                kept2[ck, i] = (kept1[ck, own, i].astype(F32) + got1[ck, i].astype(F32)).astype(BF)
        else:
            total = kept2[ck, own].astype(F32) + got2[ck].astype(F32)
            out[ck * RC : ck * RC + RC, first : first + width] = total.astype(BF)

    q_load.wait()
    d_load.wait()
    row = lax.broadcasted_iota(jnp.int32, (256, 256), 0)
    col = lax.broadcasted_iota(jnp.int32, (256, 256), 1)
    split = jnp.where(
        col == lax.rem(row // 16, 2) * 128 + row // 32 * 16 + lax.rem(row, 16), 1.0, 0.0
    ).astype(BF)
    for k in range(4):
        lane = slice(k * 256, k * 256 + 256)
        q_part = exact_dot(qbuf[:, lane], split).astype(BF)
        gated_part = exact_dot(gated[:, lane], split)
        left = jnp.broadcast_to(skip[:, lane], (16, 256))
        skip_part = jnp.zeros((16, 256), F32)
        for _ in range(3):
            term = left.astype(BF)
            left = left - term.astype(F32)
            skip_part = skip_part + exact_dot(term, split)
        for g in range(2):
            half = slice(g * 128, g * 128 + 128)
            to = slice(k * 128, k * 128 + 128)
            for ck in range(2):
                for i in range(Q):
                    at = i * R + ck * RC
                    rows = slice(ck * 128 + i * RC, ck * 128 + i * RC + RC)
                    q_own[g, rows, to] = q_part[at : at + RC, half]
                    direct[g, rows, to] = skip_part[:, half] * gated_part[at : at + RC, half]

    def mix(field, g, ck, count):
        for i in range(Q):
            rows = slice(ck * 128 + i * RC, ck * 128 + i * RC + RC)
            for o in range(4):
                lane = slice(o * 128, o * 128 + 128)
                at = o * count + (ck * RC if count == R else 0)
                conv = field[at : at + RC, PLACE[i] * 128 : PLACE[i] * 128 + 128]
                mixed[g, rows, lane] = (
                    q_own[g, rows, lane].astype(F32) * (conv + direct[g, rows, lane])
                ).astype(BF)

    waiter(y0send, y0recv, y_sem.at[0]).wait_recv()
    for e in range(CTX):
        o, i = e // 8, e % 8
        stage[o * R : o * R + R, i * 128 : i * 128 + 128] = y0recv[e]
    field = exact_dot(stage[:128, :], swap[...])
    for ck in range(2):
        mix(field, 0, ck, R)
    w_loads[0].wait()
    w_loads[1].wait()

    @pl.loop(0, OUT // 512)
    def _(n):
        cols = pl.ds(pl.multiple_of(n * 512, 512), 512)
        zacc[:, cols] = exact_dot(mixed[0], wbuf[0, :, :, cols].reshape(512, 512))

    for ck in range(2):
        waiter(y1send.at[ck], y1recv.at[ck], y_sem.at[1 + ck]).wait_recv()
        for e in range(CTX):
            o, i = e // 8, e % 8
            stage[o * RC : o * RC + RC, i * 128 : i * 128 + 128] = y1recv[ck, e]
        field = exact_dot(stage[:64, :], swap[...])
        mix(field, 1, ck, RC)
        chunk = slice(ck * 128, ck * 128 + 128)
        for t, (first, width, ways) in enumerate(ROUTES):
            whole = sums[6 * t]

            @pl.loop(0, width // 256)
            def _(n):
                at = pl.multiple_of(n * 256, 256)
                cols = pl.ds(at + first, 256)
                part = exact_dot(mixed[1, chunk, :], wbuf[1, :, :, cols].reshape(512, 256))
                part = (part + zacc[chunk, cols]).astype(BF)
                for p in range(8):
                    to = [bit(p, way) for way in ways]
                    whole[ck, to[0], to[1], to[2], :, pl.ds(at, 256)] = part[p * RC : p * RC + RC]

            hop(ck, t, 0).start()

    for step in range(3):
        for ck in range(2):
            for t in range(3):
                add_up(ck, t, step)
                if step < 2:
                    hop(ck, t, step + 1).start()

    waiter(fsend, frecv, f_sem).wait_send()
    waiter(y0send, y0recv, y_sem.at[0]).wait_send()
    for i in range(2):
        waiter(xsend.at[i], xrecv.at[i], x_sem.at[i]).wait_send()
        waiter(y1send.at[i], y1recv.at[i], y_sem.at[1 + i]).wait_send()
        for t in range(3):
            for step in range(3):
                hop(i, t, step).wait_send()


def shards(q_proj, k_proj, v_proj, filters, lengths, skip_gain, out_weight):
    swap = jnp.asarray(lane_swap(), BF)
    vmem = pl.BlockSpec(memory_space=pltpu.VMEM)
    hbm = pl.BlockSpec(memory_space=pl.ANY)
    dma = pltpu.SemaphoreType.DMA
    sums = []
    for _, width, _ in ROUTES:
        for lead in ((2, 2, 2), (2, 2), (2, 2), (2,), (2,), ()):
            sums.append(pltpu.VMEM((2,) + lead + (RC, width), BF))
    scratch = [
        pltpu.VMEM((TOK, CH), BF),
        pltpu.VMEM((TOK, CH), BF),
        pltpu.VMEM((TOK, CH), BF),
        pltpu.VMEM((GRP, TOK), F32),
        pltpu.VMEM((2, CTX, C16, OUT), BF),
        pltpu.VMEM((CH, CH), BF),
        pltpu.VMEM((1, GRP), jnp.int32),
        pltpu.VMEM((1, CH), F32),
        pltpu.VMEM((TOK, CH), BF),
        pltpu.VMEM((TOK, CH), BF),
        pltpu.VMEM((CTX, 4, 128), F32),
        pltpu.VMEM((CTX, 4, 128), F32),
        pltpu.VMEM((2, CTX, R, 128), BF),
        pltpu.VMEM((2, CTX, R, 128), BF),
        pltpu.VMEM((8, WIDE), F32),
        pltpu.VMEM((2, TOK, SEQ), BF),
        pltpu.VMEM((TOK, 640), BF),
        pltpu.VMEM((8 * TOK, 512), BF),
        pltpu.VMEM((TOK, 512), F32),
        pltpu.VMEM((CTX, R, 128), BF),
        pltpu.VMEM((CTX, R, 128), BF),
        pltpu.VMEM((2, CTX, RC, 128), BF),
        pltpu.VMEM((2, CTX, RC, 128), BF),
        pltpu.VMEM((2, TOK, 512), BF),
        pltpu.VMEM((2, TOK, 512), F32),
        pltpu.VMEM((2, TOK, 512), BF),
        pltpu.VMEM((TOK, OUT), F32),
        *sums,
        dma((9,)),
        dma((2,)),
        dma((2, 2)),
        dma((3, 2)),
        dma((18,)),
        dma((18,)),
    ]
    return pl.pallas_call(
        kernel,
        out_shape=jax.ShapeDtypeStruct((R, OUT), BF),
        in_specs=[hbm] * 8,
        out_specs=vmem,
        scratch_shapes=scratch,
        compiler_params=pltpu.CompilerParams(
            collective_id=0, has_side_effects=True, vmem_limit_bytes=56 << 20
        ),
        name="hyena",
    )(
        k_proj, v_proj, q_proj, filters.T, out_weight.reshape(CTX, 2, C16, OUT), swap,
        lengths.reshape(1, GRP), skip_gain.reshape(1, CH),
    )


def solution(mesh):
    return jax.shard_map(
        shards,
        mesh=mesh,
        in_specs=(
            P("ctx", "tp"),
            P("ctx", "tp"),
            P("ctx", "tp"),
            P("ctx", "tp"),
            P("tp"),
            P("tp"),
            P("tp", None),
        ),
        out_specs=P(("ctx", "tp"), None),
        check_vma=False,
    )
```

```python
import functools

import jax
import jax.numpy as jnp
import numpy as np
from jax import lax
from jax.experimental import pallas as pl
from jax.experimental.pallas import tpu as pltpu
from jax.sharding import PartitionSpec as P

MESH = pl.DeviceIdType.MESH
BF = jnp.bfloat16
F32 = jnp.float32

CTX = 32
TOK = 256
CH = 1024
GRP = 64
C16 = 16
OUT = 4096
R = 32
Q = 8
RC = R // 2
SEQ = CTX * TOK
WIDE = SEQ + 256

ORDER = (0, 2, 4, 6, 1, 3, 5, 7)
PLACE = tuple(ORDER.index(i) for i in range(8))


ROUTES = (
    (0, 768, ("x0", "x1", "z")),
    (768, 768, ("x1", "z", "x0")),
    (1536, 768, ("z", "x0", "x1")),
    (2304, 512, ("x0", "x1", "z")),
    (2816, 768, ("x1", "z", "x0")),
    (3584, 512, ("z", "x0", "x1")),
)
NR = len(ROUTES)


def bit(tp, way):
    x = tp % 4
    if way == "z":
        return tp // 4
    return x // 2 if way == "x1" else (x + 1) // 2 % 2


def lane_swap():
    swap = np.zeros((8, 8, 16, 8, 8, 16), np.float32)
    for a in range(8):
        for b in range(8):
            for c in range(16):
                swap[a, b, c, PLACE[b], a, c] = 1.0
    return swap.reshape(CH, CH)


def exact_dot(left, right):
    return jnp.dot(left, right, preferred_element_type=F32)


def kernel(
    k_hbm, v_hbm, q_hbm, f_hbm, w_hbm, s_hbm, l_hbm, d_hbm, out,
    kbuf, vbuf, qbuf, fbuf, wbuf, swap, lens, skip, gated, stage,
    fsend, frecv, xsend, xrecv, wide, turned, toep, xpad, xv, yacc, y0send, y0recv, y1send, y1recv, q_own, direct, field0, mixed, zacc,
    *rest,
):
    sums, (obuf, load_sem, f_sem, x_sem, y_sem, rs_send, rs_recv, out_sem) = rest[:-8], rest[-8:]
    me = lax.axis_index("ctx")
    tp = lax.axis_index("tp")
    zl, x = tp // 4, lax.rem(tp, 4)
    mine = {"x0": lax.rem((x + 1) // 2, 2), "x1": x // 2, "z": zl}
    partner = {
        "x0": {"tp": zl * 4 + x + 1 - 2 * lax.rem(x, 2)},
        "x1": {"tp": zl * 4 + 3 - x},
        "z": {"tp": (1 - zl) * 4 + x},
    }

    def load(source, target, index):
        copy = pltpu.make_async_copy(source, target, load_sem.at[index])
        copy.start()
        return copy

    k_load = load(k_hbm, kbuf, 0)
    v_load = load(v_hbm, vbuf, 1)
    s_load = load(s_hbm, swap, 2)
    f_load = load(f_hbm, fbuf, 3)
    l_load = load(l_hbm, lens, 4)
    d_load = load(d_hbm, skip, 5)

    barrier = pltpu.get_barrier_semaphore()

    @pl.loop(1, CTX)
    def _(step):
        pl.semaphore_signal(
            barrier, inc=1, device_id={"ctx": lax.rem(me + step, CTX)}, device_id_type=MESH
        )

    for way in ("x0", "x1", "z"):
        pl.semaphore_signal(barrier, inc=1, device_id=partner[way], device_id_type=MESH)

    def send_all(source, target, sems):
        for far in (2, 1, 3, 0):

            @pl.loop(0 if far else 1, 8)
            def _(near):
                e = lax.rem(me // 8 + far, 4) * 8
                e += lax.rem(me // 2 + near // 2, 4) * 2 + lax.rem(me + near, 2)
                pltpu.make_async_remote_copy(
                    source.at[e], target.at[me], sems.at[0], sems.at[1],
                    device_id={"ctx": e}, device_id_type=MESH,
                ).start()

    def waiter(source, target, sems):
        return pltpu.make_async_remote_copy(
            source.at[pl.ds(0, CTX - 1)], target.at[pl.ds(0, CTX - 1)], sems.at[0], sems.at[1],
            device_id={"ctx": lax.rem(me + 1, CTX)}, device_id_type=MESH,
        )

    k_load.wait()
    v_load.wait()
    for i in range(Q):
        part = (kbuf[i * R : i * R + R].astype(F32) * vbuf[i * R : i * R + R].astype(F32)).astype(BF)
        gated[i * R : i * R + R] = part
        for o in range(8):
            stage[o * R : o * R + R, i * 128 : i * 128 + 128] = part[:, o * 128 : o * 128 + 128]
    f_load.wait()
    l_load.wait()
    row = lax.broadcasted_iota(jnp.int32, (GRP, GRP), 0)
    col = lax.broadcasted_iota(jnp.int32, (GRP, GRP), 1)
    limit = jnp.sum(jnp.where(row == col, lens[...].astype(F32), 0.0), axis=1, keepdims=True)
    lag = (me * TOK + lax.broadcasted_iota(jnp.int32, (GRP, TOK), 1)).astype(F32)
    taps = jnp.where(lag < limit, fbuf[...], 0.0).astype(BF)
    row = lax.broadcasted_iota(jnp.int32, (TOK, TOK), 0)
    col = lax.broadcasted_iota(jnp.int32, (TOK, TOK), 1)
    flip = jnp.where(row + col == TOK - 1, 1.0, 0.0).astype(BF)
    back = exact_dot(taps, flip).astype(BF)
    row = lax.broadcasted_iota(jnp.int32, (128, GRP), 0)
    col = lax.broadcasted_iota(jnp.int32, (128, GRP), 1)
    rows = None
    for half in range(2):
        pick = jnp.where(row == 2 * col + half, 1.0, 0.0).astype(BF)
        part = exact_dot(pick, back[:, half * 128 : half * 128 + 128])
        rows = part if rows is None else rows + part
    for e in range(CTX):
        fsend[e] = rows[4 * e : 4 * e + 4]
    frecv[me] = fsend[me]

    s_load.wait()

    def send_group(g):
        packed = exact_dot(stage[...], swap[:, g * 512 : g * 512 + 512]).astype(BF)
        for o in range(8):
            for i in range(4):
                xsend[g, o * 4 + i] = packed[o * R : o * R + R, i * 128 : i * 128 + 128]
        xrecv[g, me] = xsend[g, me]
        if g == 0:
            pl.semaphore_wait(barrier, CTX - 1 + 3)
            send_all(fsend, frecv, f_sem)
        send_all(xsend.at[g], xrecv.at[g], x_sem.at[g])

    send_group(0)

    send_group(1)
    q_load = load(q_hbm, qbuf, 6)
    w_loads = [load(w_hbm.at[:, g], wbuf.at[g], 7 + g) for g in range(2)]
    waiter(fsend, frecv, f_sem).wait_recv()
    for g in range(2):
        for n in range(2 * CTX):
            tap_row = frecv[CTX - 1 - n // 2, g * 2 + n % 2 : g * 2 + n % 2 + 1, :]
            wide[:, n * 128 : n * 128 + 128] = jnp.broadcast_to(tap_row, (16, 128))
        wide[:, SEQ:] = jnp.zeros((16, WIDE - SEQ), F32)
        turned[...] = pltpu.roll(wide[...], WIDE - 15, 1, stride=1, stride_axis=0).astype(BF)

        @pl.loop(0, 8)
        def _(a):
            both = pltpu.roll(turned[...], WIDE - 112 + 16 * a, 1)
            at = pl.multiple_of(lax.rem(a, 2) * 128 + a // 2 * 16, 16)
            toep[g, pl.ds(at + 64, 16), :] = both[:, :SEQ]
            toep[g, pl.ds(at, 16), :] = both[:, 128 : SEQ + 128]

    def split_groups():
        q_load.wait()
        d_load.wait()
        row = lax.broadcasted_iota(jnp.int32, (256, 256), 0)
        col = lax.broadcasted_iota(jnp.int32, (256, 256), 1)
        split = jnp.where(
            col == lax.rem(row // 16, 2) * 128 + row // 32 * 16 + lax.rem(row, 16), 1.0, 0.0
        ).astype(BF)
        for k in range(4):
            lane = slice(k * 256, k * 256 + 256)
            q_part = exact_dot(qbuf[:, lane], split).astype(BF)
            gated_part = exact_dot(gated[:, lane], split)
            left = jnp.broadcast_to(skip[:, lane], (16, 256))
            skip_part = jnp.zeros((16, 256), F32)
            for _ in range(3):
                term = left.astype(BF)
                left = left - term.astype(F32)
                skip_part = skip_part + exact_dot(term, split)
            for g in range(2):
                half = slice(g * 128, g * 128 + 128)
                to = slice(k * 128, k * 128 + 128)
                for ck in range(2):
                    for i in range(Q):
                        at = i * R + ck * RC
                        rows = slice(ck * 128 + i * RC, ck * 128 + i * RC + RC)
                        q_own[g, rows, to] = q_part[at : at + RC, half]
                        direct[g, rows, to] = skip_part[:, half] * gated_part[at : at + RC, half]

    xpad[:, :128] = jnp.zeros((TOK, 128), BF)
    for g in range(2):
        waiter(xsend.at[g], xrecv.at[g], x_sem.at[g]).wait_recv()
        for b in range(CTX):
            stage[(b // 8) * R : (b // 8) * R + R, (b % 8) * 128 : (b % 8) * 128 + 128] = xrecv[g, b]
        blocks = exact_dot(stage[:128, :], swap[...]).astype(BF)
        for o in range(4):
            for i in range(Q):
                xpad[i * R : i * R + R, 128 + o * 128 : 256 + o * 128] = blocks[
                    o * R : o * R + R, PLACE[i] * 128 : PLACE[i] * 128 + 128
                ]
        for n in range(8):
            moved = xpad[...]
            if n < 7:
                moved = pltpu.roll(moved, 16 * (7 - n), 1)
            xv[n * TOK : n * TOK + TOK, :] = moved[:, 128:]
        def convolve(rows):
            yacc[rows] = exact_dot(toep[g, rows, 24 * TOK :], xv[...])
            for d in range(1, 4):
                width = 512 - 128 * d
                part = exact_dot(toep[g, rows, (24 - 8 * d) * TOK : (32 - 8 * d) * TOK], xv[:, :width])
                yacc[rows, 128 * d :] = yacc[rows, 128 * d :] + part

        def pack(ck, start):
            for o in range(4):
                for i in range(Q):
                    at = ck * 128 + i * RC
                    to = start + o * RC
                    stage[to : to + RC, i * 128 : i * 128 + 128] = yacc[
                        at : at + RC, o * 128 : o * 128 + 128
                    ].astype(BF)

        if g == 0:
            convolve(slice(0, TOK))
            pack(0, 0)
            pack(1, 64)
            packed = exact_dot(stage[:128, :], swap[...]).astype(BF)
            for ck in range(2):
                for b in range(CTX):
                    at = ck * 64 + (b // 8) * RC
                    lane = PLACE[b % 8] * 128
                    y0send[b, ck * RC : ck * RC + RC] = packed[at : at + RC, lane : lane + 128]
            y0recv[me] = y0send[me]
            send_all(y0send, y0recv, y_sem.at[0])
            split_groups()
        else:
            for ck in range(2):
                convolve(slice(ck * 128, ck * 128 + 128))
                pack(ck, 0)
                packed = exact_dot(stage[:64, :], swap[...]).astype(BF)
                for b in range(CTX):
                    at = (b // 8) * RC
                    lane = PLACE[b % 8] * 128
                    y1send[ck, b] = packed[at : at + RC, lane : lane + 128]
                y1recv[ck, me] = y1send[ck, me]
                send_all(y1send.at[ck], y1recv.at[ck], y_sem.at[1 + ck])

    def hop(ck, t, step):
        whole, got0, kept1, got1, kept2, got2 = sums[6 * t : 6 * t + 6]
        way = ROUTES[t][2][step]
        source = (whole, kept1, kept2)[step].at[ck, 1 - mine[way]]
        target = (got0, got1, got2)[step].at[ck]
        index = (ck * NR + t) * 3 + step
        return pltpu.make_async_remote_copy(
            source, target, rs_send.at[index], rs_recv.at[index],
            device_id=partner[way], device_id_type=MESH,
        )

    def store(ck, t):
        first, width, _ = ROUTES[t]
        return pltpu.make_async_copy(
            obuf.at[ck, :, pl.ds(first, width)],
            out.at[pl.ds(ck * RC, RC), pl.ds(first, width)],
            out_sem.at[ck * NR + t],
        )

    def add_up(ck, t, step):
        whole, got0, kept1, got1, kept2, got2 = sums[6 * t : 6 * t + 6]
        first, width, ways = ROUTES[t]
        own = mine[ways[step]]
        hop(ck, t, step).wait_recv()
        if step == 0:
            for i in range(2):
                for j in range(2):
                    kept1[ck, i, j] = (whole[ck, own, i, j].astype(F32) + got0[ck, i, j].astype(F32)).astype(BF)
        elif step == 1:
            for i in range(2):
                kept2[ck, i] = (kept1[ck, own, i].astype(F32) + got1[ck, i].astype(F32)).astype(BF)
        else:
            total = kept2[ck, own].astype(F32) + got2[ck].astype(F32)
            obuf[ck, :, first : first + width] = total.astype(BF)
            store(ck, t).start()

    def mix(field, g, ck, count):
        for i in range(Q):
            rows = slice(ck * 128 + i * RC, ck * 128 + i * RC + RC)
            for o in range(4):
                lane = slice(o * 128, o * 128 + 128)
                at = o * count + (ck * RC if count == R else 0)
                conv = field[at : at + RC, PLACE[i] * 128 : PLACE[i] * 128 + 128]
                mixed[g, rows, lane] = (
                    q_own[g, rows, lane].astype(F32) * (conv + direct[g, rows, lane])
                ).astype(BF)

    waiter(y0send, y0recv, y_sem.at[0]).wait_recv()
    for e in range(CTX):
        o, i = e // 8, e % 8
        stage[o * R : o * R + R, i * 128 : i * 128 + 128] = y0recv[e]
    field0[...] = exact_dot(stage[:128, :], swap[...])
    w_loads[0].wait()
    w_loads[1].wait()

    def project_first(ck):
        mix(field0, 0, ck, R)
        chunk = slice(ck * 128, ck * 128 + 128)

        @pl.loop(0, OUT // 512)
        def _(n):
            cols = pl.ds(pl.multiple_of(n * 512, 512), 512)
            zacc[chunk, cols] = exact_dot(mixed[0, chunk, :], wbuf[0, :, :, cols].reshape(512, 512))

    for ck in range(2):
        project_first(ck)
        waiter(y1send.at[ck], y1recv.at[ck], y_sem.at[1 + ck]).wait_recv()
        for e in range(CTX):
            o, i = e // 8, e % 8
            stage[o * RC : o * RC + RC, i * 128 : i * 128 + 128] = y1recv[ck, e]
        field = exact_dot(stage[:64, :], swap[...])
        mix(field, 1, ck, RC)
        chunk = slice(ck * 128, ck * 128 + 128)
        for t, (first, width, ways) in enumerate(ROUTES):
            whole = sums[6 * t]

            @pl.loop(0, width // 256)
            def _(n):
                at = pl.multiple_of(n * 256, 256)
                cols = pl.ds(at + first, 256)
                part = exact_dot(mixed[1, chunk, :], wbuf[1, :, :, cols].reshape(512, 256))
                part = (part + zacc[chunk, cols]).astype(BF)
                for p in range(8):
                    to = [bit(p, way) for way in ways]
                    whole[ck, to[0], to[1], to[2], :, pl.ds(at, 256)] = part[p * RC : p * RC + RC]

            hop(ck, t, 0).start()

    for step in range(3):
        for ck in range(2):
            for t in range(NR):
                add_up(ck, t, step)
                if step < 2:
                    hop(ck, t, step + 1).start()

    waiter(fsend, frecv, f_sem).wait_send()
    waiter(y0send, y0recv, y_sem.at[0]).wait_send()
    for i in range(2):
        waiter(xsend.at[i], xrecv.at[i], x_sem.at[i]).wait_send()
        waiter(y1send.at[i], y1recv.at[i], y_sem.at[1 + i]).wait_send()
        for t in range(NR):
            for step in range(3):
                hop(i, t, step).wait_send()
            store(i, t).wait()


def shards(q_proj, k_proj, v_proj, filters, lengths, skip_gain, out_weight):
    swap = jnp.asarray(lane_swap(), BF)
    hbm = pl.BlockSpec(memory_space=pl.ANY)
    dma = pltpu.SemaphoreType.DMA
    sums = []
    for _, width, _ in ROUTES:
        for lead in ((2, 2, 2), (2, 2), (2, 2), (2,), (2,), ()):
            sums.append(pltpu.VMEM((2,) + lead + (RC, width), BF))
    scratch = [
        pltpu.VMEM((TOK, CH), BF),
        pltpu.VMEM((TOK, CH), BF),
        pltpu.VMEM((TOK, CH), BF),
        pltpu.VMEM((GRP, TOK), F32),
        pltpu.VMEM((2, CTX, C16, OUT), BF),
        pltpu.VMEM((CH, CH), BF),
        pltpu.VMEM((1, GRP), jnp.int32),
        pltpu.VMEM((1, CH), F32),
        pltpu.VMEM((TOK, CH), BF),
        pltpu.VMEM((TOK, CH), BF),
        pltpu.VMEM((CTX, 4, 128), F32),
        pltpu.VMEM((CTX, 4, 128), F32),
        pltpu.VMEM((2, CTX, R, 128), BF),
        pltpu.VMEM((2, CTX, R, 128), BF),
        pltpu.VMEM((16, WIDE), F32),
        pltpu.VMEM((16, WIDE), BF),
        pltpu.VMEM((2, TOK, SEQ), BF),
        pltpu.VMEM((TOK, 640), BF),
        pltpu.VMEM((8 * TOK, 512), BF),
        pltpu.VMEM((TOK, 512), F32),
        pltpu.VMEM((CTX, R, 128), BF),
        pltpu.VMEM((CTX, R, 128), BF),
        pltpu.VMEM((2, CTX, RC, 128), BF),
        pltpu.VMEM((2, CTX, RC, 128), BF),
        pltpu.VMEM((2, TOK, 512), BF),
        pltpu.VMEM((2, TOK, 512), F32),
        pltpu.VMEM((128, CH), F32),
        pltpu.VMEM((2, TOK, 512), BF),
        pltpu.VMEM((TOK, OUT), F32),
        *sums,
        pltpu.VMEM((2, RC, OUT), BF),
        dma((9,)),
        dma((2,)),
        dma((2, 2)),
        dma((3, 2)),
        dma((6 * NR,)),
        dma((6 * NR,)),
        dma((2 * NR,)),
    ]
    return pl.pallas_call(
        kernel,
        out_shape=jax.ShapeDtypeStruct((R, OUT), BF),
        in_specs=[hbm] * 8,
        out_specs=hbm,
        scratch_shapes=scratch,
        compiler_params=pltpu.CompilerParams(
            collective_id=0, has_side_effects=True, vmem_limit_bytes=56 << 20
        ),
        name="hyena",
    )(
        k_proj, v_proj, q_proj, filters.T, out_weight.reshape(CTX, 2, C16, OUT), swap,
        lengths.reshape(1, GRP), skip_gain.reshape(1, CH),
    )


def solution(mesh):
    return jax.shard_map(
        shards,
        mesh=mesh,
        in_specs=(
            P("ctx", "tp"),
            P("ctx", "tp"),
            P("ctx", "tp"),
            P("ctx", "tp"),
            P("tp"),
            P("tp"),
            P("tp", None),
        ),
        out_specs=P(("ctx", "tp"), None),
        check_vma=False,
    )
```

```python
import functools

import jax
import jax.numpy as jnp
import numpy as np
from jax import lax
from jax.experimental import pallas as pl
from jax.experimental.pallas import tpu as pltpu
from jax.sharding import PartitionSpec as P

MESH = pl.DeviceIdType.MESH
BF = jnp.bfloat16
F32 = jnp.float32

CTX = 32
TOK = 256
CH = 1024
GRP = 64
C16 = 16
OUT = 4096
R = 32
Q = 8
RC = R // 2
SEQ = CTX * TOK
WIDE = SEQ + 256

ORDER = (0, 2, 4, 6, 1, 3, 5, 7)
PLACE = tuple(ORDER.index(i) for i in range(8))


ROUTES = (
    (0, 768, ("x0", "x1", "z")),
    (768, 768, ("x1", "z", "x0")),
    (1536, 768, ("z", "x0", "x1")),
    (2304, 512, ("x0", "x1", "z")),
    (2816, 768, ("x1", "z", "x0")),
    (3584, 512, ("z", "x0", "x1")),
)
NR = len(ROUTES)


def bit(tp, way):
    x = tp % 4
    if way == "z":
        return tp // 4
    return x // 2 if way == "x1" else (x + 1) // 2 % 2


def lane_swap():
    swap = np.zeros((8, 8, 16, 8, 8, 16), np.float32)
    for a in range(8):
        for b in range(8):
            for c in range(16):
                swap[a, b, c, PLACE[b], a, c] = 1.0
    return swap.reshape(CH, CH)


def exact_dot(left, right):
    return jnp.dot(left, right, preferred_element_type=F32)


def kernel(
    k_hbm, v_hbm, q_hbm, f_hbm, w_hbm, s_hbm, l_hbm, d_hbm, out,
    kbuf, vbuf, qbuf, fbuf, wbuf, swap, lens, skip, gated, stage,
    fsend, frecv, xsend, xrecv, wide, turned, toep, xpad, xv, yacc, y0send, y0recv, y1send, y1recv, q_own, direct, field0, mixed, zacc,
    *rest,
):
    sums, (obuf, load_sem, f_sem, x_sem, y_sem, rs_send, rs_recv, out_sem) = rest[:-8], rest[-8:]
    me = lax.axis_index("ctx")
    tp = lax.axis_index("tp")
    zl, x = tp // 4, lax.rem(tp, 4)
    mine = {"x0": lax.rem((x + 1) // 2, 2), "x1": x // 2, "z": zl}
    partner = {
        "x0": {"tp": zl * 4 + x + 1 - 2 * lax.rem(x, 2)},
        "x1": {"tp": zl * 4 + 3 - x},
        "z": {"tp": (1 - zl) * 4 + x},
    }

    def load(source, target, index):
        copy = pltpu.make_async_copy(source, target, load_sem.at[index])
        copy.start()
        return copy

    k_load = load(k_hbm, kbuf, 0)
    v_load = load(v_hbm, vbuf, 1)
    s_load = load(s_hbm, swap, 2)
    f_load = load(f_hbm, fbuf, 3)
    l_load = load(l_hbm, lens, 4)
    d_load = load(d_hbm, skip, 5)

    barrier = pltpu.get_barrier_semaphore()

    @pl.loop(1, CTX)
    def _(step):
        pl.semaphore_signal(
            barrier, inc=1, device_id={"ctx": lax.rem(me + step, CTX)}, device_id_type=MESH
        )

    for way in ("x0", "x1", "z"):
        pl.semaphore_signal(barrier, inc=1, device_id=partner[way], device_id_type=MESH)

    def send_all(source, target, sems):
        for far in (2, 1, 3, 0):

            @pl.loop(0 if far else 1, 8)
            def _(near):
                e = lax.rem(me // 8 + far, 4) * 8
                e += lax.rem(me // 2 + near // 2, 4) * 2 + lax.rem(me + near, 2)
                pltpu.make_async_remote_copy(
                    source.at[e], target.at[me], sems.at[0], sems.at[1],
                    device_id={"ctx": e}, device_id_type=MESH,
                ).start()

    def waiter(source, target, sems):
        return pltpu.make_async_remote_copy(
            source.at[pl.ds(0, CTX - 1)], target.at[pl.ds(0, CTX - 1)], sems.at[0], sems.at[1],
            device_id={"ctx": lax.rem(me + 1, CTX)}, device_id_type=MESH,
        )

    k_load.wait()
    v_load.wait()
    for i in range(Q):
        part = (kbuf[i * R : i * R + R].astype(F32) * vbuf[i * R : i * R + R].astype(F32)).astype(BF)
        gated[i * R : i * R + R] = part
        for o in range(8):
            stage[o * R : o * R + R, i * 128 : i * 128 + 128] = part[:, o * 128 : o * 128 + 128]
    f_load.wait()
    l_load.wait()
    row = lax.broadcasted_iota(jnp.int32, (GRP, GRP), 0)
    col = lax.broadcasted_iota(jnp.int32, (GRP, GRP), 1)
    limit = jnp.sum(jnp.where(row == col, lens[...].astype(F32), 0.0), axis=1, keepdims=True)
    lag = (me * TOK + lax.broadcasted_iota(jnp.int32, (GRP, TOK), 1)).astype(F32)
    taps = jnp.where(lag < limit, fbuf[...], 0.0).astype(BF)
    row = lax.broadcasted_iota(jnp.int32, (TOK, TOK), 0)
    col = lax.broadcasted_iota(jnp.int32, (TOK, TOK), 1)
    flip = jnp.where(row + col == TOK - 1, 1.0, 0.0).astype(BF)
    back = exact_dot(taps, flip).astype(BF)
    row = lax.broadcasted_iota(jnp.int32, (128, GRP), 0)
    col = lax.broadcasted_iota(jnp.int32, (128, GRP), 1)
    rows = None
    for half in range(2):
        pick = jnp.where(row == 2 * col + half, 1.0, 0.0).astype(BF)
        part = exact_dot(pick, back[:, half * 128 : half * 128 + 128])
        rows = part if rows is None else rows + part
    for e in range(CTX):
        fsend[e] = rows[4 * e : 4 * e + 4]
    frecv[me] = fsend[me]

    s_load.wait()

    def send_group(g):
        packed = exact_dot(stage[...], swap[:, g * 512 : g * 512 + 512]).astype(BF)
        for o in range(8):
            for i in range(4):
                xsend[g, o * 4 + i] = packed[o * R : o * R + R, i * 128 : i * 128 + 128]
        xrecv[g, me] = xsend[g, me]
        if g == 0:
            pl.semaphore_wait(barrier, CTX - 1 + 3)
            send_all(fsend, frecv, f_sem)
        send_all(xsend.at[g], xrecv.at[g], x_sem.at[g])

    send_group(0)

    send_group(1)
    q_load = load(q_hbm, qbuf, 6)
    w_loads = [load(w_hbm.at[:, g], wbuf.at[g], 7 + g) for g in range(2)]
    waiter(fsend, frecv, f_sem).wait_recv()
    for g in range(2):
        for n in range(2 * CTX):
            tap_row = frecv[CTX - 1 - n // 2, g * 2 + n % 2 : g * 2 + n % 2 + 1, :]
            wide[:, n * 128 : n * 128 + 128] = jnp.broadcast_to(tap_row, (16, 128))
        wide[:, SEQ:] = jnp.zeros((16, WIDE - SEQ), F32)
        turned[...] = pltpu.roll(wide[...], WIDE - 15, 1, stride=1, stride_axis=0).astype(BF)

        @pl.loop(0, 8)
        def _(a):
            both = pltpu.roll(turned[...], WIDE - 112 + 16 * a, 1)
            at = pl.multiple_of(lax.rem(a, 2) * 128 + a // 2 * 16, 16)
            toep[g, pl.ds(at + 64, 16), :] = both[:, :SEQ]
            toep[g, pl.ds(at, 16), :] = both[:, 128 : SEQ + 128]

    def split_groups():
        q_load.wait()
        d_load.wait()
        row = lax.broadcasted_iota(jnp.int32, (256, 256), 0)
        col = lax.broadcasted_iota(jnp.int32, (256, 256), 1)
        split = jnp.where(
            col == lax.rem(row // 16, 2) * 128 + row // 32 * 16 + lax.rem(row, 16), 1.0, 0.0
        ).astype(BF)
        for k in range(4):
            lane = slice(k * 256, k * 256 + 256)
            q_part = exact_dot(qbuf[:, lane], split).astype(BF)
            gated_part = exact_dot(gated[:, lane], split)
            left = jnp.broadcast_to(skip[:, lane], (16, 256))
            skip_part = jnp.zeros((16, 256), F32)
            for _ in range(3):
                term = left.astype(BF)
                left = left - term.astype(F32)
                skip_part = skip_part + exact_dot(term, split)
            for g in range(2):
                half = slice(g * 128, g * 128 + 128)
                to = slice(k * 128, k * 128 + 128)
                for ck in range(2):
                    for i in range(Q):
                        at = i * R + ck * RC
                        rows = slice(ck * 128 + i * RC, ck * 128 + i * RC + RC)
                        q_own[g, rows, to] = q_part[at : at + RC, half]
                        direct[g, rows, to] = skip_part[:, half] * gated_part[at : at + RC, half]

    xpad[:, :128] = jnp.zeros((TOK, 128), BF)
    for g in range(2):
        waiter(xsend.at[g], xrecv.at[g], x_sem.at[g]).wait_recv()
        for b in range(CTX):
            stage[(b // 8) * R : (b // 8) * R + R, (b % 8) * 128 : (b % 8) * 128 + 128] = xrecv[g, b]
        blocks = exact_dot(stage[:128, :], swap[...]).astype(BF)
        for o in range(4):
            for i in range(Q):
                xpad[i * R : i * R + R, 128 + o * 128 : 256 + o * 128] = blocks[
                    o * R : o * R + R, PLACE[i] * 128 : PLACE[i] * 128 + 128
                ]
        for n in range(8):
            moved = xpad[...]
            if n < 7:
                moved = pltpu.roll(moved, 16 * (7 - n), 1)
            xv[n * TOK : n * TOK + TOK, :] = moved[:, 128:]
        def convolve(rows):
            yacc[rows] = exact_dot(toep[g, rows, 24 * TOK :], xv[...])
            for d in range(1, 4):
                width = 512 - 128 * d
                part = exact_dot(toep[g, rows, (24 - 8 * d) * TOK : (32 - 8 * d) * TOK], xv[:, :width])
                yacc[rows, 128 * d :] = yacc[rows, 128 * d :] + part

        def pack(ck, start):
            for o in range(4):
                for i in range(Q):
                    at = ck * 128 + i * RC
                    to = start + o * RC
                    stage[to : to + RC, i * 128 : i * 128 + 128] = yacc[
                        at : at + RC, o * 128 : o * 128 + 128
                    ].astype(BF)

        if g == 0:
            convolve(slice(0, TOK))
            pack(0, 0)
            pack(1, 64)
            packed = exact_dot(stage[:128, :], swap[...]).astype(BF)
            for ck in range(2):
                for b in range(CTX):
                    at = ck * 64 + (b // 8) * RC
                    lane = PLACE[b % 8] * 128
                    y0send[b, ck * RC : ck * RC + RC] = packed[at : at + RC, lane : lane + 128]
            y0recv[me] = y0send[me]
            send_all(y0send, y0recv, y_sem.at[0])
            split_groups()
        else:
            for ck in range(2):
                convolve(slice(ck * 128, ck * 128 + 128))
                pack(ck, 0)
                packed = exact_dot(stage[:64, :], swap[...]).astype(BF)
                for b in range(CTX):
                    at = (b // 8) * RC
                    lane = PLACE[b % 8] * 128
                    y1send[ck, b] = packed[at : at + RC, lane : lane + 128]
                y1recv[ck, me] = y1send[ck, me]
                send_all(y1send.at[ck], y1recv.at[ck], y_sem.at[1 + ck])

    def hop(ck, t, step):
        whole, got0, kept1, got1, kept2, got2 = sums[6 * t : 6 * t + 6]
        way = ROUTES[t][2][step]
        source = (whole, kept1, kept2)[step].at[ck, 1 - mine[way]]
        target = (got0, got1, got2)[step].at[ck]
        index = (ck * NR + t) * 3 + step
        return pltpu.make_async_remote_copy(
            source, target, rs_send.at[index], rs_recv.at[index],
            device_id=partner[way], device_id_type=MESH,
        )

    def store(ck, t):
        first, width, _ = ROUTES[t]
        return pltpu.make_async_copy(
            obuf.at[ck, :, pl.ds(first, width)],
            out.at[pl.ds(ck * RC, RC), pl.ds(first, width)],
            out_sem.at[ck * NR + t],
        )

    def add_up(ck, t, step):
        whole, got0, kept1, got1, kept2, got2 = sums[6 * t : 6 * t + 6]
        first, width, ways = ROUTES[t]
        own = mine[ways[step]]
        hop(ck, t, step).wait_recv()
        if step == 0:
            for i in range(2):
                for j in range(2):
                    kept1[ck, i, j] = (whole[ck, own, i, j].astype(F32) + got0[ck, i, j].astype(F32)).astype(BF)
        elif step == 1:
            for i in range(2):
                kept2[ck, i] = (kept1[ck, own, i].astype(F32) + got1[ck, i].astype(F32)).astype(BF)
        else:
            total = kept2[ck, own].astype(F32) + got2[ck].astype(F32)
            obuf[ck, :, first : first + width] = total.astype(BF)
            store(ck, t).start()

    def mix(field, g, ck, count):
        for i in range(Q):
            rows = slice(ck * 128 + i * RC, ck * 128 + i * RC + RC)
            for o in range(4):
                lane = slice(o * 128, o * 128 + 128)
                at = o * count + (ck * RC if count == R else 0)
                conv = field[at : at + RC, PLACE[i] * 128 : PLACE[i] * 128 + 128]
                mixed[g, rows, lane] = (
                    q_own[g, rows, lane].astype(F32) * (conv + direct[g, rows, lane])
                ).astype(BF)

    waiter(y0send, y0recv, y_sem.at[0]).wait_recv()
    for e in range(CTX):
        o, i = e // 8, e % 8
        stage[o * R : o * R + R, i * 128 : i * 128 + 128] = y0recv[e]
    field0[...] = exact_dot(stage[:128, :], swap[...])
    w_loads[0].wait()
    w_loads[1].wait()

    def project_first(ck):
        mix(field0, 0, ck, R)
        chunk = slice(ck * 128, ck * 128 + 128)

        for n in range(0, OUT, 1024):
            cols = slice(n, n + 1024)
            zacc[chunk, cols] = exact_dot(mixed[0, chunk, :], wbuf[0, :, :, cols].reshape(512, 1024))

    for ck in range(2):
        project_first(ck)
        waiter(y1send.at[ck], y1recv.at[ck], y_sem.at[1 + ck]).wait_recv()
        for e in range(CTX):
            o, i = e // 8, e % 8
            stage[o * RC : o * RC + RC, i * 128 : i * 128 + 128] = y1recv[ck, e]
        field = exact_dot(stage[:64, :], swap[...])
        mix(field, 1, ck, RC)
        chunk = slice(ck * 128, ck * 128 + 128)
        for t, (first, width, ways) in enumerate(ROUTES):
            whole = sums[6 * t]
            cols = slice(first, first + width)
            part = exact_dot(mixed[1, chunk, :], wbuf[1, :, :, cols].reshape(512, width))
            part = (part + zacc[chunk, cols]).astype(BF)
            for p in range(8):
                to = [bit(p, way) for way in ways]
                whole[ck, to[0], to[1], to[2]] = part[p * RC : p * RC + RC]

            hop(ck, t, 0).start()

    for step in range(3):
        for ck in range(2):
            for t in range(NR):
                add_up(ck, t, step)
                if step < 2:
                    hop(ck, t, step + 1).start()

    waiter(fsend, frecv, f_sem).wait_send()
    waiter(y0send, y0recv, y_sem.at[0]).wait_send()
    for i in range(2):
        waiter(xsend.at[i], xrecv.at[i], x_sem.at[i]).wait_send()
        waiter(y1send.at[i], y1recv.at[i], y_sem.at[1 + i]).wait_send()
        for t in range(NR):
            for step in range(3):
                hop(i, t, step).wait_send()
            store(i, t).wait()


def shards(q_proj, k_proj, v_proj, filters, lengths, skip_gain, out_weight):
    swap = jnp.asarray(lane_swap(), BF)
    hbm = pl.BlockSpec(memory_space=pl.ANY)
    dma = pltpu.SemaphoreType.DMA
    sums = []
    for _, width, _ in ROUTES:
        for lead in ((2, 2, 2), (2, 2), (2, 2), (2,), (2,), ()):
            sums.append(pltpu.VMEM((2,) + lead + (RC, width), BF))
    scratch = [
        pltpu.VMEM((TOK, CH), BF),
        pltpu.VMEM((TOK, CH), BF),
        pltpu.VMEM((TOK, CH), BF),
        pltpu.VMEM((GRP, TOK), F32),
        pltpu.VMEM((2, CTX, C16, OUT), BF),
        pltpu.VMEM((CH, CH), BF),
        pltpu.VMEM((1, GRP), jnp.int32),
        pltpu.VMEM((1, CH), F32),
        pltpu.VMEM((TOK, CH), BF),
        pltpu.VMEM((TOK, CH), BF),
        pltpu.VMEM((CTX, 4, 128), F32),
        pltpu.VMEM((CTX, 4, 128), F32),
        pltpu.VMEM((2, CTX, R, 128), BF),
        pltpu.VMEM((2, CTX, R, 128), BF),
        pltpu.VMEM((16, WIDE), F32),
        pltpu.VMEM((16, WIDE), BF),
        pltpu.VMEM((2, TOK, SEQ), BF),
        pltpu.VMEM((TOK, 640), BF),
        pltpu.VMEM((8 * TOK, 512), BF),
        pltpu.VMEM((TOK, 512), F32),
        pltpu.VMEM((CTX, R, 128), BF),
        pltpu.VMEM((CTX, R, 128), BF),
        pltpu.VMEM((2, CTX, RC, 128), BF),
        pltpu.VMEM((2, CTX, RC, 128), BF),
        pltpu.VMEM((2, TOK, 512), BF),
        pltpu.VMEM((2, TOK, 512), F32),
        pltpu.VMEM((128, CH), F32),
        pltpu.VMEM((2, TOK, 512), BF),
        pltpu.VMEM((TOK, OUT), F32),
        *sums,
        pltpu.VMEM((2, RC, OUT), BF),
        dma((9,)),
        dma((2,)),
        dma((2, 2)),
        dma((3, 2)),
        dma((6 * NR,)),
        dma((6 * NR,)),
        dma((2 * NR,)),
    ]
    return pl.pallas_call(
        kernel,
        out_shape=jax.ShapeDtypeStruct((R, OUT), BF),
        in_specs=[hbm] * 8,
        out_specs=hbm,
        scratch_shapes=scratch,
        compiler_params=pltpu.CompilerParams(
            collective_id=0, has_side_effects=True, vmem_limit_bytes=56 << 20
        ),
        name="hyena",
    )(
        k_proj, v_proj, q_proj, filters.T, out_weight.reshape(CTX, 2, C16, OUT), swap,
        lengths.reshape(1, GRP), skip_gain.reshape(1, CH),
    )


def solution(mesh):
    return jax.shard_map(
        shards,
        mesh=mesh,
        in_specs=(
            P("ctx", "tp"),
            P("ctx", "tp"),
            P("ctx", "tp"),
            P("ctx", "tp"),
            P("tp"),
            P("tp"),
            P("tp", None),
        ),
        out_specs=P(("ctx", "tp"), None),
        check_vma=False,
    )
```

```python
import functools

import jax
import jax.numpy as jnp
import numpy as np
from jax import lax
from jax.experimental import pallas as pl
from jax.experimental.pallas import tpu as pltpu
from jax.sharding import PartitionSpec as P

MESH = pl.DeviceIdType.MESH
BF = jnp.bfloat16
F32 = jnp.float32

CTX = 32
TOK = 256
CH = 1024
GRP = 64
C16 = 16
OUT = 4096
R = 32
Q = 8
RC = R // 2
SEQ = CTX * TOK
WIDE = SEQ + 256

ORDER = (0, 2, 4, 6, 1, 3, 5, 7)
PLACE = tuple(ORDER.index(i) for i in range(8))


ROUTES = (
    (0, 768, ("x0", "x1", "z")),
    (768, 768, ("x1", "z", "x0")),
    (1536, 640, ("z", "x0", "x1")),
    (2176, 640, ("x0", "x1", "z")),
    (2816, 640, ("x1", "z", "x0")),
    (3456, 640, ("z", "x0", "x1")),
)
NR = len(ROUTES)


def bit(tp, way):
    x = tp % 4
    if way == "z":
        return tp // 4
    return x // 2 if way == "x1" else (x + 1) // 2 % 2


def lane_swap():
    swap = np.zeros((8, 8, 16, 8, 8, 16), np.float32)
    for a in range(8):
        for b in range(8):
            for c in range(16):
                swap[a, b, c, PLACE[b], a, c] = 1.0
    return swap.reshape(CH, CH)


def exact_dot(left, right):
    return jnp.dot(left, right, preferred_element_type=F32)


def kernel(
    k_hbm, v_hbm, q_hbm, f_hbm, w_hbm, s_hbm, l_hbm, d_hbm, out, brought,
    kbuf, vbuf, qbuf, fbuf, wbuf, swap, lens, skip, gated, stage,
    fsend, frecv, xsend, xrecv, wide, turned, toep, xpad, xv, yacc, y0send, y0recv, y1send, y1recv, q_own, direct, field0, mixed, zacc,
    *rest,
):
    sums, (load_sem, f_sem, x_sem, y_sem, rs_send, rs_recv, out_sem) = rest[:-7], rest[-7:]
    me = lax.axis_index("ctx")
    tp = lax.axis_index("tp")
    zl, x = tp // 4, lax.rem(tp, 4)
    mine = {"x0": lax.rem((x + 1) // 2, 2), "x1": x // 2, "z": zl}
    partner = {
        "x0": {"tp": zl * 4 + x + 1 - 2 * lax.rem(x, 2)},
        "x1": {"tp": zl * 4 + 3 - x},
        "z": {"tp": (1 - zl) * 4 + x},
    }

    def load(source, target, index):
        copy = pltpu.make_async_copy(source, target, load_sem.at[index])
        copy.start()
        return copy

    k_load = load(k_hbm, kbuf, 0)
    v_load = load(v_hbm, vbuf, 1)
    s_load = load(s_hbm, swap, 2)
    f_load = load(f_hbm, fbuf, 3)
    l_load = load(l_hbm, lens, 4)
    d_load = load(d_hbm, skip, 5)

    barrier = pltpu.get_barrier_semaphore()

    @pl.loop(1, CTX)
    def _(step):
        pl.semaphore_signal(
            barrier, inc=1, device_id={"ctx": lax.rem(me + step, CTX)}, device_id_type=MESH
        )

    for way in ("x0", "x1", "z"):
        pl.semaphore_signal(barrier, inc=1, device_id=partner[way], device_id_type=MESH)

    def send_all(source, target, sems):
        for far in (2, 1, 3, 0):

            @pl.loop(0 if far else 1, 8)
            def _(near):
                e = lax.rem(me // 8 + far, 4) * 8
                e += lax.rem(me // 2 + near // 2, 4) * 2 + lax.rem(me + near, 2)
                pltpu.make_async_remote_copy(
                    source.at[e], target.at[me], sems.at[0], sems.at[1],
                    device_id={"ctx": e}, device_id_type=MESH,
                ).start()

    def waiter(source, target, sems):
        return pltpu.make_async_remote_copy(
            source.at[pl.ds(0, CTX - 1)], target.at[pl.ds(0, CTX - 1)], sems.at[0], sems.at[1],
            device_id={"ctx": lax.rem(me + 1, CTX)}, device_id_type=MESH,
        )

    k_load.wait()
    v_load.wait()
    for i in range(Q):
        part = (kbuf[i * R : i * R + R].astype(F32) * vbuf[i * R : i * R + R].astype(F32)).astype(BF)
        gated[i * R : i * R + R] = part
        for o in range(8):
            stage[o * R : o * R + R, i * 128 : i * 128 + 128] = part[:, o * 128 : o * 128 + 128]
    f_load.wait()
    l_load.wait()
    row = lax.broadcasted_iota(jnp.int32, (GRP, GRP), 0)
    col = lax.broadcasted_iota(jnp.int32, (GRP, GRP), 1)
    limit = jnp.sum(jnp.where(row == col, lens[...].astype(F32), 0.0), axis=1, keepdims=True)
    lag = (me * TOK + lax.broadcasted_iota(jnp.int32, (GRP, TOK), 1)).astype(F32)
    taps = jnp.where(lag < limit, fbuf[...], 0.0).astype(BF)
    row = lax.broadcasted_iota(jnp.int32, (TOK, TOK), 0)
    col = lax.broadcasted_iota(jnp.int32, (TOK, TOK), 1)
    flip = jnp.where(row + col == TOK - 1, 1.0, 0.0).astype(BF)
    back = exact_dot(taps, flip).astype(BF)
    row = lax.broadcasted_iota(jnp.int32, (128, GRP), 0)
    col = lax.broadcasted_iota(jnp.int32, (128, GRP), 1)
    rows = None
    for half in range(2):
        pick = jnp.where(row == 2 * col + half, 1.0, 0.0).astype(BF)
        part = exact_dot(pick, back[:, half * 128 : half * 128 + 128])
        rows = part if rows is None else rows + part
    for e in range(CTX):
        fsend[e] = rows[4 * e : 4 * e + 4]
    frecv[me] = fsend[me]

    s_load.wait()

    def send_group(g):
        packed = exact_dot(stage[...], swap[:, g * 512 : g * 512 + 512]).astype(BF)
        for o in range(8):
            for i in range(4):
                xsend[g, o * 4 + i] = packed[o * R : o * R + R, i * 128 : i * 128 + 128]
        xrecv[g, me] = xsend[g, me]
        if g == 0:
            pl.semaphore_wait(barrier, CTX - 1 + 3)
            send_all(fsend, frecv, f_sem)
        send_all(xsend.at[g], xrecv.at[g], x_sem.at[g])

    send_group(0)

    send_group(1)
    q_load = load(q_hbm, qbuf, 6)
    w_loads = [load(w_hbm.at[:, g], wbuf.at[g], 7 + g) for g in range(2)]
    waiter(fsend, frecv, f_sem).wait_recv()
    for g in range(2):
        for n in range(2 * CTX):
            tap_row = frecv[CTX - 1 - n // 2, g * 2 + n % 2 : g * 2 + n % 2 + 1, :]
            wide[:, n * 128 : n * 128 + 128] = jnp.broadcast_to(tap_row, (16, 128))
        wide[:, SEQ:] = jnp.zeros((16, WIDE - SEQ), F32)
        turned[...] = pltpu.roll(wide[...], WIDE - 15, 1, stride=1, stride_axis=0).astype(BF)

        @pl.loop(0, 8)
        def _(a):
            both = pltpu.roll(turned[...], WIDE - 112 + 16 * a, 1)
            at = pl.multiple_of(lax.rem(a, 2) * 128 + a // 2 * 16, 16)
            toep[g, pl.ds(at + 64, 16), :] = both[:, :SEQ]
            toep[g, pl.ds(at, 16), :] = both[:, 128 : SEQ + 128]

    def split_groups():
        q_load.wait()
        d_load.wait()
        row = lax.broadcasted_iota(jnp.int32, (256, 256), 0)
        col = lax.broadcasted_iota(jnp.int32, (256, 256), 1)
        split = jnp.where(
            col == lax.rem(row // 16, 2) * 128 + row // 32 * 16 + lax.rem(row, 16), 1.0, 0.0
        ).astype(BF)
        for k in range(4):
            lane = slice(k * 256, k * 256 + 256)
            q_part = exact_dot(qbuf[:, lane], split).astype(BF)
            gated_part = exact_dot(gated[:, lane], split)
            left = jnp.broadcast_to(skip[:, lane], (16, 256))
            skip_part = jnp.zeros((16, 256), F32)
            for _ in range(3):
                term = left.astype(BF)
                left = left - term.astype(F32)
                skip_part = skip_part + exact_dot(term, split)
            for g in range(2):
                half = slice(g * 128, g * 128 + 128)
                to = slice(k * 128, k * 128 + 128)
                for ck in range(2):
                    for i in range(Q):
                        at = i * R + ck * RC
                        rows = slice(ck * 128 + i * RC, ck * 128 + i * RC + RC)
                        q_own[g, rows, to] = q_part[at : at + RC, half]
                        direct[g, rows, to] = skip_part[:, half] * gated_part[at : at + RC, half]

    xpad[:, :128] = jnp.zeros((TOK, 128), BF)
    for g in range(2):
        waiter(xsend.at[g], xrecv.at[g], x_sem.at[g]).wait_recv()
        for b in range(CTX):
            stage[(b // 8) * R : (b // 8) * R + R, (b % 8) * 128 : (b % 8) * 128 + 128] = xrecv[g, b]
        blocks = exact_dot(stage[:128, :], swap[...]).astype(BF)
        for o in range(4):
            for i in range(Q):
                xpad[i * R : i * R + R, 128 + o * 128 : 256 + o * 128] = blocks[
                    o * R : o * R + R, PLACE[i] * 128 : PLACE[i] * 128 + 128
                ]
        for n in range(8):
            moved = xpad[...]
            if n < 7:
                moved = pltpu.roll(moved, 16 * (7 - n), 1)
            xv[n * TOK : n * TOK + TOK, :] = moved[:, 128:]
        def convolve(rows):
            yacc[rows] = exact_dot(toep[g, rows, 24 * TOK :], xv[...])
            for d in range(1, 4):
                width = 512 - 128 * d
                part = exact_dot(toep[g, rows, (24 - 8 * d) * TOK : (32 - 8 * d) * TOK], xv[:, :width])
                yacc[rows, 128 * d :] = yacc[rows, 128 * d :] + part

        def pack(ck, start):
            for o in range(4):
                for i in range(Q):
                    at = ck * 128 + i * RC
                    to = start + o * RC
                    stage[to : to + RC, i * 128 : i * 128 + 128] = yacc[
                        at : at + RC, o * 128 : o * 128 + 128
                    ].astype(BF)

        if g == 0:
            convolve(slice(0, TOK))
            pack(0, 0)
            pack(1, 64)
            packed = exact_dot(stage[:128, :], swap[...]).astype(BF)
            for ck in range(2):
                for b in range(CTX):
                    at = ck * 64 + (b // 8) * RC
                    lane = PLACE[b % 8] * 128
                    y0send[b, ck * RC : ck * RC + RC] = packed[at : at + RC, lane : lane + 128]
            y0recv[me] = y0send[me]
            send_all(y0send, y0recv, y_sem.at[0])
            split_groups()
        else:
            for ck in range(2):
                convolve(slice(ck * 128, ck * 128 + 128))
                pack(ck, 0)
                packed = exact_dot(stage[:64, :], swap[...]).astype(BF)
                for b in range(CTX):
                    at = (b // 8) * RC
                    lane = PLACE[b % 8] * 128
                    y1send[ck, b] = packed[at : at + RC, lane : lane + 128]
                y1recv[ck, me] = y1send[ck, me]
                send_all(y1send.at[ck], y1recv.at[ck], y_sem.at[1 + ck])

    def piece(whole, ck, t):
        first, width, _ = ROUTES[t]
        return whole.at[pl.ds(ck * RC, RC), pl.ds(first, width)]

    def hop(ck, t, step):
        whole, got0, kept1, got1, kept2 = sums[5 * t : 5 * t + 5]
        way = ROUTES[t][2][step]
        source = (whole, kept1, kept2)[step].at[ck, 1 - mine[way]]
        target = (got0, got1)[step].at[ck] if step < 2 else piece(brought, ck, t)
        index = (ck * NR + t) * 3 + step
        return pltpu.make_async_remote_copy(
            source, target, rs_send.at[index], rs_recv.at[index],
            device_id=partner[way], device_id_type=MESH,
        )

    def store(ck, t):
        kept2 = sums[5 * t + 4]
        return pltpu.make_async_copy(
            kept2.at[ck, mine[ROUTES[t][2][2]]], piece(out, ck, t), out_sem.at[ck * NR + t]
        )

    def add_up(ck, t, step):
        whole, got0, kept1, got1, kept2 = sums[5 * t : 5 * t + 5]
        own = mine[ROUTES[t][2][step]]
        hop(ck, t, step).wait_recv()
        if step == 0:
            for i in range(2):
                for j in range(2):
                    kept1[ck, i, j] = (whole[ck, own, i, j].astype(F32) + got0[ck, i, j].astype(F32)).astype(BF)
        elif step == 1:
            for i in range(2):
                kept2[ck, i] = (kept1[ck, own, i].astype(F32) + got1[ck, i].astype(F32)).astype(BF)
            store(ck, t).start()

    def mix(field, g, ck, count):
        for i in range(Q):
            rows = slice(ck * 128 + i * RC, ck * 128 + i * RC + RC)
            for o in range(4):
                lane = slice(o * 128, o * 128 + 128)
                at = o * count + (ck * RC if count == R else 0)
                conv = field[at : at + RC, PLACE[i] * 128 : PLACE[i] * 128 + 128]
                mixed[g, rows, lane] = (
                    q_own[g, rows, lane].astype(F32) * (conv + direct[g, rows, lane])
                ).astype(BF)

    waiter(y0send, y0recv, y_sem.at[0]).wait_recv()
    for e in range(CTX):
        o, i = e // 8, e % 8
        stage[o * R : o * R + R, i * 128 : i * 128 + 128] = y0recv[e]
    field0[...] = exact_dot(stage[:128, :], swap[...])
    w_loads[0].wait()
    w_loads[1].wait()

    def project_first(ck):
        mix(field0, 0, ck, R)
        chunk = slice(ck * 128, ck * 128 + 128)

        for n in range(0, OUT, 1024):
            cols = slice(n, n + 1024)
            zacc[chunk, cols] = exact_dot(mixed[0, chunk, :], wbuf[0, :, :, cols].reshape(512, 1024))

    for ck in range(2):
        project_first(ck)
        waiter(y1send.at[ck], y1recv.at[ck], y_sem.at[1 + ck]).wait_recv()
        for e in range(CTX):
            o, i = e // 8, e % 8
            stage[o * RC : o * RC + RC, i * 128 : i * 128 + 128] = y1recv[ck, e]
        field = exact_dot(stage[:64, :], swap[...])
        mix(field, 1, ck, RC)
        chunk = slice(ck * 128, ck * 128 + 128)
        for t, (first, width, ways) in enumerate(ROUTES):
            whole = sums[5 * t]
            cols = slice(first, first + width)
            part = exact_dot(mixed[1, chunk, :], wbuf[1, :, :, cols].reshape(512, width))
            part = (part + zacc[chunk, cols]).astype(BF)
            for p in range(8):
                to = [bit(p, way) for way in ways]
                whole[ck, to[0], to[1], to[2]] = part[p * RC : p * RC + RC]

            hop(ck, t, 0).start()

    for step in range(3):
        for ck in range(2):
            for t in range(NR):
                add_up(ck, t, step)
                if step < 2:
                    hop(ck, t, step + 1).start()

    waiter(fsend, frecv, f_sem).wait_send()
    waiter(y0send, y0recv, y_sem.at[0]).wait_send()
    for i in range(2):
        waiter(xsend.at[i], xrecv.at[i], x_sem.at[i]).wait_send()
        waiter(y1send.at[i], y1recv.at[i], y_sem.at[1 + i]).wait_send()
        for t in range(NR):
            for step in range(3):
                hop(i, t, step).wait_send()
            store(i, t).wait()


def shards(q_proj, k_proj, v_proj, filters, lengths, skip_gain, out_weight):
    swap = jnp.asarray(lane_swap(), BF)
    hbm = pl.BlockSpec(memory_space=pl.ANY)
    dma = pltpu.SemaphoreType.DMA
    sums = []
    for _, width, _ in ROUTES:
        for lead in ((2, 2, 2), (2, 2), (2, 2), (2,), (2,)):
            sums.append(pltpu.VMEM((2,) + lead + (RC, width), BF))
    scratch = [
        pltpu.VMEM((TOK, CH), BF),
        pltpu.VMEM((TOK, CH), BF),
        pltpu.VMEM((TOK, CH), BF),
        pltpu.VMEM((GRP, TOK), F32),
        pltpu.VMEM((2, CTX, C16, OUT), BF),
        pltpu.VMEM((CH, CH), BF),
        pltpu.VMEM((1, GRP), jnp.int32),
        pltpu.VMEM((1, CH), F32),
        pltpu.VMEM((TOK, CH), BF),
        pltpu.VMEM((TOK, CH), BF),
        pltpu.VMEM((CTX, 4, 128), F32),
        pltpu.VMEM((CTX, 4, 128), F32),
        pltpu.VMEM((2, CTX, R, 128), BF),
        pltpu.VMEM((2, CTX, R, 128), BF),
        pltpu.VMEM((16, WIDE), F32),
        pltpu.VMEM((16, WIDE), BF),
        pltpu.VMEM((2, TOK, SEQ), BF),
        pltpu.VMEM((TOK, 640), BF),
        pltpu.VMEM((8 * TOK, 512), BF),
        pltpu.VMEM((TOK, 512), F32),
        pltpu.VMEM((CTX, R, 128), BF),
        pltpu.VMEM((CTX, R, 128), BF),
        pltpu.VMEM((2, CTX, RC, 128), BF),
        pltpu.VMEM((2, CTX, RC, 128), BF),
        pltpu.VMEM((2, TOK, 512), BF),
        pltpu.VMEM((2, TOK, 512), F32),
        pltpu.VMEM((128, CH), F32),
        pltpu.VMEM((2, TOK, 512), BF),
        pltpu.VMEM((TOK, OUT), F32),
        *sums,
        dma((9,)),
        dma((2,)),
        dma((2, 2)),
        dma((3, 2)),
        dma((6 * NR,)),
        dma((6 * NR,)),
        dma((2 * NR,)),
    ]
    kept, brought = pl.pallas_call(
        kernel,
        out_shape=[jax.ShapeDtypeStruct((R, OUT), BF)] * 2,
        in_specs=[hbm] * 8,
        out_specs=[hbm] * 2,
        scratch_shapes=scratch,
        compiler_params=pltpu.CompilerParams(
            collective_id=0, has_side_effects=True, vmem_limit_bytes=56 << 20
        ),
        name="hyena",
    )(
        k_proj, v_proj, q_proj, filters.T, out_weight.reshape(CTX, 2, C16, OUT), swap,
        lengths.reshape(1, GRP), skip_gain.reshape(1, CH),
    )
    return (kept.astype(F32) + brought.astype(F32)).astype(BF)


def solution(mesh):
    return jax.shard_map(
        shards,
        mesh=mesh,
        in_specs=(
            P("ctx", "tp"),
            P("ctx", "tp"),
            P("ctx", "tp"),
            P("ctx", "tp"),
            P("tp"),
            P("tp"),
            P("tp", None),
        ),
        out_specs=P(("ctx", "tp"), None),
        check_vma=False,
    )
```

```python
import functools

import jax
import jax.numpy as jnp
import numpy as np
from jax import lax
from jax.experimental import pallas as pl
from jax.experimental.pallas import tpu as pltpu
from jax.sharding import PartitionSpec as P

MESH = pl.DeviceIdType.MESH
BF = jnp.bfloat16
F32 = jnp.float32

CTX = 32
TOK = 256
CH = 1024
GRP = 64
C16 = 16
OUT = 4096
R = 32
Q = 8
RC = R // 2
SEQ = CTX * TOK
WIDE = SEQ + 256

ORDER = (0, 2, 4, 6, 1, 3, 5, 7)
PLACE = tuple(ORDER.index(i) for i in range(8))


ROUTES = (
    (0, 768, ("x0", "x1", "z")),
    (768, 768, ("x1", "z", "x0")),
    (1536, 640, ("z", "x0", "x1")),
    (2176, 640, ("x0", "x1", "z")),
    (2816, 640, ("x1", "z", "x0")),
    (3456, 640, ("z", "x0", "x1")),
)
NR = len(ROUTES)


def bit(tp, way):
    x = tp % 4
    if way == "z":
        return tp // 4
    return x // 2 if way == "x1" else (x + 1) // 2 % 2


def lane_swap():
    swap = np.zeros((8, 8, 16, 8, 8, 16), np.float32)
    for a in range(8):
        for b in range(8):
            for c in range(16):
                swap[a, b, c, PLACE[b], a, c] = 1.0
    return swap.reshape(CH, CH)


def exact_dot(left, right):
    return jnp.dot(left, right, preferred_element_type=F32)


def kernel(
    k_hbm, v_hbm, q_hbm, f_hbm, w_hbm, s_hbm, l_hbm, d_hbm, out, brought,
    kbuf, vbuf, qbuf, fbuf, wbuf, swap, lens, skip, gated, stage,
    fsend, frecv, xsend, xrecv, wide, turned, toep, xpad, xv, yacc, y0send, y0recv, y1send, y1recv, q_own, direct, field0, mixed, zacc,
    *rest,
):
    sums, (load_sem, f_sem, x_sem, y_sem, rs_send, rs_recv, out_sem) = rest[:-7], rest[-7:]
    me = lax.axis_index("ctx")
    tp = lax.axis_index("tp")
    zl, x = tp // 4, lax.rem(tp, 4)
    mine = {"x0": lax.rem((x + 1) // 2, 2), "x1": x // 2, "z": zl}
    partner = {
        "x0": {"tp": zl * 4 + x + 1 - 2 * lax.rem(x, 2)},
        "x1": {"tp": zl * 4 + 3 - x},
        "z": {"tp": (1 - zl) * 4 + x},
    }

    def load(source, target, index):
        copy = pltpu.make_async_copy(source, target, load_sem.at[index])
        copy.start()
        return copy

    k_load = load(k_hbm, kbuf, 0)
    v_load = load(v_hbm, vbuf, 1)
    s_load = load(s_hbm, swap, 2)
    f_load = load(f_hbm, fbuf, 3)
    l_load = load(l_hbm, lens, 4)
    d_load = load(d_hbm, skip, 5)

    barrier = pltpu.get_barrier_semaphore()

    @pl.loop(1, CTX)
    def _(step):
        pl.semaphore_signal(
            barrier, inc=1, device_id={"ctx": lax.rem(me + step, CTX)}, device_id_type=MESH
        )

    for way in ("x0", "x1", "z"):
        pl.semaphore_signal(barrier, inc=1, device_id=partner[way], device_id_type=MESH)

    def send_all(source, target, sems):
        for far in (2, 1, 3, 0):

            @pl.loop(0 if far else 1, 8)
            def _(near):
                e = lax.rem(me // 8 + far, 4) * 8
                e += lax.rem(me // 2 + near // 2, 4) * 2 + lax.rem(me + near, 2)
                pltpu.make_async_remote_copy(
                    source.at[e], target.at[me], sems.at[0], sems.at[1],
                    device_id={"ctx": e}, device_id_type=MESH,
                ).start()

    def waiter(source, target, sems):
        return pltpu.make_async_remote_copy(
            source.at[pl.ds(0, CTX - 1)], target.at[pl.ds(0, CTX - 1)], sems.at[0], sems.at[1],
            device_id={"ctx": lax.rem(me + 1, CTX)}, device_id_type=MESH,
        )

    k_load.wait()
    v_load.wait()
    for i in range(Q):
        part = (kbuf[i * R : i * R + R].astype(F32) * vbuf[i * R : i * R + R].astype(F32)).astype(BF)
        gated[i * R : i * R + R] = part
        for o in range(8):
            stage[o * R : o * R + R, i * 128 : i * 128 + 128] = part[:, o * 128 : o * 128 + 128]
    f_load.wait()
    l_load.wait()
    row = lax.broadcasted_iota(jnp.int32, (GRP, GRP), 0)
    col = lax.broadcasted_iota(jnp.int32, (GRP, GRP), 1)
    limit = jnp.sum(jnp.where(row == col, lens[...].astype(F32), 0.0), axis=1, keepdims=True)
    lag = (me * TOK + lax.broadcasted_iota(jnp.int32, (GRP, TOK), 1)).astype(F32)
    taps = jnp.where(lag < limit, fbuf[...], 0.0).astype(BF)
    row = lax.broadcasted_iota(jnp.int32, (TOK, TOK), 0)
    col = lax.broadcasted_iota(jnp.int32, (TOK, TOK), 1)
    flip = jnp.where(row + col == TOK - 1, 1.0, 0.0).astype(BF)
    back = exact_dot(taps, flip).astype(BF)
    row = lax.broadcasted_iota(jnp.int32, (128, GRP), 0)
    col = lax.broadcasted_iota(jnp.int32, (128, GRP), 1)
    rows = None
    for half in range(2):
        pick = jnp.where(row == 2 * col + half, 1.0, 0.0).astype(BF)
        part = exact_dot(pick, back[:, half * 128 : half * 128 + 128])
        rows = part if rows is None else rows + part
    for e in range(CTX):
        fsend[e] = rows[4 * e : 4 * e + 4]
    frecv[me] = fsend[me]

    s_load.wait()

    def send_group(g):
        packed = exact_dot(stage[...], swap[:, g * 512 : g * 512 + 512]).astype(BF)
        for o in range(8):
            for i in range(4):
                xsend[g, o * 4 + i] = packed[o * R : o * R + R, i * 128 : i * 128 + 128]
        xrecv[g, me] = xsend[g, me]
        if g == 0:
            pl.semaphore_wait(barrier, CTX - 1 + 3)
            send_all(fsend, frecv, f_sem)
        send_all(xsend.at[g], xrecv.at[g], x_sem.at[g])

    send_group(0)

    send_group(1)
    q_load = load(q_hbm, qbuf, 6)
    w_loads = [load(w_hbm.at[:, g], wbuf.at[g], 7 + g) for g in range(2)]
    waiter(fsend, frecv, f_sem).wait_recv()

    def build(g):
        for n in range(2 * CTX):
            tap_row = frecv[CTX - 1 - n // 2, g * 2 + n % 2 : g * 2 + n % 2 + 1, :]
            wide[:, n * 128 : n * 128 + 128] = jnp.broadcast_to(tap_row, (16, 128))
        wide[:, SEQ:] = jnp.zeros((16, WIDE - SEQ), F32)
        turned[...] = pltpu.roll(wide[...], WIDE - 15, 1, stride=1, stride_axis=0).astype(BF)

        @pl.loop(0, 8)
        def _(a):
            both = pltpu.roll(turned[...], WIDE - 112 + 16 * a, 1)
            at = pl.multiple_of(lax.rem(a, 2) * 128 + a // 2 * 16, 16)
            toep[g, pl.ds(at + 64, 16), :] = both[:, :SEQ]
            toep[g, pl.ds(at, 16), :] = both[:, 128 : SEQ + 128]

    def split_groups():
        q_load.wait()
        d_load.wait()
        row = lax.broadcasted_iota(jnp.int32, (256, 256), 0)
        col = lax.broadcasted_iota(jnp.int32, (256, 256), 1)
        split = jnp.where(
            col == lax.rem(row // 16, 2) * 128 + row // 32 * 16 + lax.rem(row, 16), 1.0, 0.0
        ).astype(BF)
        for k in range(4):
            lane = slice(k * 256, k * 256 + 256)
            q_part = exact_dot(qbuf[:, lane], split).astype(BF)
            gated_part = exact_dot(gated[:, lane], split)
            left = jnp.broadcast_to(skip[:, lane], (16, 256))
            skip_part = jnp.zeros((16, 256), F32)
            for _ in range(3):
                term = left.astype(BF)
                left = left - term.astype(F32)
                skip_part = skip_part + exact_dot(term, split)
            for g in range(2):
                half = slice(g * 128, g * 128 + 128)
                to = slice(k * 128, k * 128 + 128)
                for ck in range(2):
                    for i in range(Q):
                        at = i * R + ck * RC
                        rows = slice(ck * 128 + i * RC, ck * 128 + i * RC + RC)
                        q_own[g, rows, to] = q_part[at : at + RC, half]
                        direct[g, rows, to] = skip_part[:, half] * gated_part[at : at + RC, half]

    xpad[:, :128] = jnp.zeros((TOK, 128), BF)
    for g in range(2):
        build(g)
        waiter(xsend.at[g], xrecv.at[g], x_sem.at[g]).wait_recv()
        for b in range(CTX):
            stage[(b // 8) * R : (b // 8) * R + R, (b % 8) * 128 : (b % 8) * 128 + 128] = xrecv[g, b]
        blocks = exact_dot(stage[:128, :], swap[...]).astype(BF)
        for o in range(4):
            for i in range(Q):
                xpad[i * R : i * R + R, 128 + o * 128 : 256 + o * 128] = blocks[
                    o * R : o * R + R, PLACE[i] * 128 : PLACE[i] * 128 + 128
                ]
        for n in range(8):
            moved = xpad[...]
            if n < 7:
                moved = pltpu.roll(moved, 16 * (7 - n), 1)
            xv[n * TOK : n * TOK + TOK, :] = moved[:, 128:]
        def convolve(rows):
            yacc[rows] = exact_dot(toep[g, rows, 24 * TOK :], xv[...])
            for d in range(1, 4):
                width = 512 - 128 * d
                part = exact_dot(toep[g, rows, (24 - 8 * d) * TOK : (32 - 8 * d) * TOK], xv[:, :width])
                yacc[rows, 128 * d :] = yacc[rows, 128 * d :] + part

        def pack(ck, start):
            for o in range(4):
                for i in range(Q):
                    at = ck * 128 + i * RC
                    to = start + o * RC
                    stage[to : to + RC, i * 128 : i * 128 + 128] = yacc[
                        at : at + RC, o * 128 : o * 128 + 128
                    ].astype(BF)

        if g == 0:
            convolve(slice(0, TOK))
            pack(0, 0)
            pack(1, 64)
            packed = exact_dot(stage[:128, :], swap[...]).astype(BF)
            for ck in range(2):
                for b in range(CTX):
                    at = ck * 64 + (b // 8) * RC
                    lane = PLACE[b % 8] * 128
                    y0send[b, ck * RC : ck * RC + RC] = packed[at : at + RC, lane : lane + 128]
            y0recv[me] = y0send[me]
            send_all(y0send, y0recv, y_sem.at[0])
        else:
            for ck in range(2):
                convolve(slice(ck * 128, ck * 128 + 128))
                pack(ck, 0)
                packed = exact_dot(stage[:64, :], swap[...]).astype(BF)
                for b in range(CTX):
                    at = (b // 8) * RC
                    lane = PLACE[b % 8] * 128
                    y1send[ck, b] = packed[at : at + RC, lane : lane + 128]
                y1recv[ck, me] = y1send[ck, me]
                send_all(y1send.at[ck], y1recv.at[ck], y_sem.at[1 + ck])

    def piece(whole, ck, t):
        first, width, _ = ROUTES[t]
        return whole.at[pl.ds(ck * RC, RC), pl.ds(first, width)]

    def hop(ck, t, step):
        whole, got0, kept1, got1, kept2 = sums[5 * t : 5 * t + 5]
        way = ROUTES[t][2][step]
        source = (whole, kept1, kept2)[step].at[ck, 1 - mine[way]]
        target = (got0, got1)[step].at[ck] if step < 2 else piece(brought, ck, t)
        index = (ck * NR + t) * 3 + step
        return pltpu.make_async_remote_copy(
            source, target, rs_send.at[index], rs_recv.at[index],
            device_id=partner[way], device_id_type=MESH,
        )

    def store(ck, t):
        kept2 = sums[5 * t + 4]
        return pltpu.make_async_copy(
            kept2.at[ck, mine[ROUTES[t][2][2]]], piece(out, ck, t), out_sem.at[ck * NR + t]
        )

    def add_up(ck, t, step):
        whole, got0, kept1, got1, kept2 = sums[5 * t : 5 * t + 5]
        own = mine[ROUTES[t][2][step]]
        hop(ck, t, step).wait_recv()
        if step == 0:
            for i in range(2):
                for j in range(2):
                    kept1[ck, i, j] = (whole[ck, own, i, j].astype(F32) + got0[ck, i, j].astype(F32)).astype(BF)
        elif step == 1:
            for i in range(2):
                kept2[ck, i] = (kept1[ck, own, i].astype(F32) + got1[ck, i].astype(F32)).astype(BF)
            store(ck, t).start()

    def mix(field, g, ck, count):
        for i in range(Q):
            rows = slice(ck * 128 + i * RC, ck * 128 + i * RC + RC)
            for o in range(4):
                lane = slice(o * 128, o * 128 + 128)
                at = o * count + (ck * RC if count == R else 0)
                conv = field[at : at + RC, PLACE[i] * 128 : PLACE[i] * 128 + 128]
                mixed[g, rows, lane] = (
                    q_own[g, rows, lane].astype(F32) * (conv + direct[g, rows, lane])
                ).astype(BF)

    split_groups()
    waiter(y0send, y0recv, y_sem.at[0]).wait_recv()
    for e in range(CTX):
        o, i = e // 8, e % 8
        stage[o * R : o * R + R, i * 128 : i * 128 + 128] = y0recv[e]
    field0[...] = exact_dot(stage[:128, :], swap[...])
    w_loads[0].wait()
    w_loads[1].wait()

    def project_first(ck):
        mix(field0, 0, ck, R)
        chunk = slice(ck * 128, ck * 128 + 128)

        for n in range(0, OUT, 1024):
            cols = slice(n, n + 1024)
            zacc[chunk, cols] = exact_dot(mixed[0, chunk, :], wbuf[0, :, :, cols].reshape(512, 1024))

    project_first(0)
    project_first(1)

    for ck in range(2):
        waiter(y1send.at[ck], y1recv.at[ck], y_sem.at[1 + ck]).wait_recv()
        for e in range(CTX):
            o, i = e // 8, e % 8
            stage[o * RC : o * RC + RC, i * 128 : i * 128 + 128] = y1recv[ck, e]
        field = exact_dot(stage[:64, :], swap[...])
        mix(field, 1, ck, RC)
        chunk = slice(ck * 128, ck * 128 + 128)
        for t, (first, width, ways) in enumerate(ROUTES):
            whole = sums[5 * t]
            cols = slice(first, first + width)
            part = exact_dot(mixed[1, chunk, :], wbuf[1, :, :, cols].reshape(512, width))
            part = (part + zacc[chunk, cols]).astype(BF)
            for p in range(8):
                to = [bit(p, way) for way in ways]
                whole[ck, to[0], to[1], to[2]] = part[p * RC : p * RC + RC]

            hop(ck, t, 0).start()

    for step in range(3):
        for ck in range(2):
            for t in range(NR):
                add_up(ck, t, step)
                if step < 2:
                    hop(ck, t, step + 1).start()

    waiter(fsend, frecv, f_sem).wait_send()
    waiter(y0send, y0recv, y_sem.at[0]).wait_send()
    for i in range(2):
        waiter(xsend.at[i], xrecv.at[i], x_sem.at[i]).wait_send()
        waiter(y1send.at[i], y1recv.at[i], y_sem.at[1 + i]).wait_send()
        for t in range(NR):
            for step in range(3):
                hop(i, t, step).wait_send()
            store(i, t).wait()


def shards(q_proj, k_proj, v_proj, filters, lengths, skip_gain, out_weight):
    swap = jnp.asarray(lane_swap(), BF)
    hbm = pl.BlockSpec(memory_space=pl.ANY)
    dma = pltpu.SemaphoreType.DMA
    sums = []
    for _, width, _ in ROUTES:
        for lead in ((2, 2, 2), (2, 2), (2, 2), (2,), (2,)):
            sums.append(pltpu.VMEM((2,) + lead + (RC, width), BF))
    scratch = [
        pltpu.VMEM((TOK, CH), BF),
        pltpu.VMEM((TOK, CH), BF),
        pltpu.VMEM((TOK, CH), BF),
        pltpu.VMEM((GRP, TOK), F32),
        pltpu.VMEM((2, CTX, C16, OUT), BF),
        pltpu.VMEM((CH, CH), BF),
        pltpu.VMEM((1, GRP), jnp.int32),
        pltpu.VMEM((1, CH), F32),
        pltpu.VMEM((TOK, CH), BF),
        pltpu.VMEM((TOK, CH), BF),
        pltpu.VMEM((CTX, 4, 128), F32),
        pltpu.VMEM((CTX, 4, 128), F32),
        pltpu.VMEM((2, CTX, R, 128), BF),
        pltpu.VMEM((2, CTX, R, 128), BF),
        pltpu.VMEM((16, WIDE), F32),
        pltpu.VMEM((16, WIDE), BF),
        pltpu.VMEM((2, TOK, SEQ), BF),
        pltpu.VMEM((TOK, 640), BF),
        pltpu.VMEM((8 * TOK, 512), BF),
        pltpu.VMEM((TOK, 512), F32),
        pltpu.VMEM((CTX, R, 128), BF),
        pltpu.VMEM((CTX, R, 128), BF),
        pltpu.VMEM((2, CTX, RC, 128), BF),
        pltpu.VMEM((2, CTX, RC, 128), BF),
        pltpu.VMEM((2, TOK, 512), BF),
        pltpu.VMEM((2, TOK, 512), F32),
        pltpu.VMEM((128, CH), F32),
        pltpu.VMEM((2, TOK, 512), BF),
        pltpu.VMEM((TOK, OUT), F32),
        *sums,
        dma((9,)),
        dma((2,)),
        dma((2, 2)),
        dma((3, 2)),
        dma((6 * NR,)),
        dma((6 * NR,)),
        dma((2 * NR,)),
    ]
    kept, brought = pl.pallas_call(
        kernel,
        out_shape=[jax.ShapeDtypeStruct((R, OUT), BF)] * 2,
        in_specs=[hbm] * 8,
        out_specs=[hbm] * 2,
        scratch_shapes=scratch,
        compiler_params=pltpu.CompilerParams(
            collective_id=0, has_side_effects=True, vmem_limit_bytes=56 << 20
        ),
        name="hyena",
    )(
        k_proj, v_proj, q_proj, filters.T, out_weight.reshape(CTX, 2, C16, OUT), swap,
        lengths.reshape(1, GRP), skip_gain.reshape(1, CH),
    )
    return (kept.astype(F32) + brought.astype(F32)).astype(BF)


def solution(mesh):
    return jax.shard_map(
        shards,
        mesh=mesh,
        in_specs=(
            P("ctx", "tp"),
            P("ctx", "tp"),
            P("ctx", "tp"),
            P("ctx", "tp"),
            P("tp"),
            P("tp"),
            P("tp", None),
        ),
        out_specs=P(("ctx", "tp"), None),
        check_vma=False,
    )
```
